256 devices in a mesh: dp: 64 (over z, x, core), group: 4 (over y).
Axes of the slice: x: 4, y: 4, z: 8, core: 2. Of those that a mesh axis runs over, the one named last changes fastest.
Arguments:
- train_grads: float32 [262144, 1024], P(('dp', 'group')), may hold values from -50 to 50
- val_grads: float32 [128, 32, 1024], P('dp', 'group'), may hold values from -6 to 6
- wanted: int32 [64, 64], replicated, may hold values from -1 to 127, as said below
- owner: int32 [64], replicated, may hold values from 0 to 63, each once
Outputs:
- scores: float32 [262144, 2048], P(('dp', 'group'))
The draws below stay inside these ranges and needn't reach their ends.
Inputs may be any that keep to these rules, and one draw needn't show every extreme that they name: wanted[b, j] is -1 or the id of a validation block stored on index j of dp, one of j * 2 to j * 2 + 1; training blocks differ in how many slots are used.
All inputs are finite; a program needn't handle non-finite values.
Results may differ from the reference program's by a relative error of at most 0.0003.
Values sent between devices are 32-bit elements; how exact they have to be, the bound alone decides.
No kernel may reach another device: no remote copies, remote signals or barrier semaphores. Data moves between devices by JAX's collectives and lax.ppermute only.
A program may use at most 128 MiB of HBM per device.

```python
import math
import jax
import jax.numpy as jnp
from jax import lax

PROJ = 1024
ROWS_DEV = 1024
VAL_DEV = 2
VB = 32
TRAIN = 262144
NVB = 128
N_DP = 64
N_GROUP = 4


def draw_train_grads(key, part):
    key = jax.random.fold_in(key, 3)
    first, second = jax.random.split(key, 2)
    column_scale = jnp.exp(jax.random.uniform(second, (1, PROJ), jnp.float32, math.log(0.3), math.log(3.0)))
    values = jax.random.normal(first, (TRAIN, PROJ), jnp.float32)
    return jnp.clip(values * column_scale, -50.0, 50.0).astype(jnp.float32)


def draw_wanted(key, part):
    key = jax.random.fold_in(key, 7)
    first, second, third = jax.random.split(key, 3)
    threshold = jax.random.randint(first, (N_DP, 1), 300, 1001)
    coin = jax.random.randint(second, (N_DP, N_DP), 0, 1000)
    within = jax.random.randint(third, (N_DP, N_DP), 0, VAL_DEV)
    base = jnp.arange(N_DP, dtype=jnp.int32)[None, :] * VAL_DEV
    return jnp.where(coin < threshold, base + within, -1).astype(jnp.int32)


def level_of(stream_key, extent, cuts, smallest, largest):
    level, own = 1.0, jax.random.fold_in(stream_key, 6)
    for dim, parts in cuts:
        draws = jnp.exp(jax.random.uniform(jax.random.fold_in(own, dim), (parts,), jnp.float32, smallest / len(cuts), largest / len(cuts)))
        level = level * jnp.repeat(draws, extent[dim] // parts).reshape([-1 if axis == dim else 1 for axis in range(len(extent))])
    return level


def centred(stream_key, shape, deviation, bound, cuts=(), kind=jnp.bfloat16):
    factor_of = level_of(stream_key, shape, cuts, -0.22, 0.18) if cuts else 1.0
    entries = jax.random.normal(stream_key, shape, jnp.float32) * deviation * factor_of
    return jnp.minimum(jnp.maximum(entries, -bound), bound).astype(kind)


def setup_inputs(seed: int = 0) -> dict:
    key_of = jax.random.split(jax.random.key(seed), 5)
    train_grads = draw_train_grads(jax.random.fold_in(key_of[4], 71), 0)
    val_grads = centred(key_of[1], (NVB, VB, PROJ), 1.0, 6.0, ((0, 64), (1, 4)), jnp.float32)
    wanted = draw_wanted(jax.random.fold_in(key_of[4], 71), 0)
    owner = jax.random.permutation(key_of[3], N_DP).astype(jnp.int32)
    return dict(train_grads=train_grads, val_grads=val_grads, wanted=wanted, owner=owner)


damping = 0.1

def cholesky_apply(factor, right_side):
    middle = lax.linalg.triangular_solve(factor, right_side, left_side=True, lower=True)
    return lax.linalg.triangular_solve(factor, middle, left_side=True, lower=True, transpose_a=True)

def reference(train_grads, val_grads, wanted, owner):
    highest = lax.Precision.HIGHEST
    gram_matrix = lax.dot_general(train_grads, train_grads, (((0,), (0,)), ((), ())), precision=highest)
    gram_matrix = gram_matrix / TRAIN + damping * jnp.eye(PROJ, dtype=jnp.float32)
    factor = jnp.linalg.cholesky(gram_matrix)
    val_rows = val_grads.reshape(NVB * VB, PROJ)
    solved = cholesky_apply(factor, val_rows.T).T.reshape(NVB, VB, PROJ)
    positions = jnp.arange(N_DP, dtype=jnp.int32)
    holder = jnp.sum(jnp.where(owner[None, :] == positions[:, None], positions[None, :], 0), axis=1).astype(jnp.int32)
    requests = wanted[holder]
    by_block = train_grads.reshape(N_DP, N_GROUP * ROWS_DEV, PROJ)
    score_scale = PROJ ** (-0.5)

    def score_tile(pair):
        block_rows, request = pair
        is_live = (request >= 0).astype(jnp.float32)
        picked = solved[jnp.maximum(request, 0).astype(jnp.int32)] * is_live[:, None, None]
        return lax.dot_general(block_rows, picked.reshape(N_DP * VB, PROJ), (((1,), (1,)), ((), ())), precision=highest) * score_scale
    result = lax.map(score_tile, (by_block, requests))
    return result.reshape(TRAIN, N_DP * VB)
```

```python
import functools
import jax
import jax.numpy as jnp
from jax import lax
from jax.experimental import pallas as pl
from jax.experimental.pallas import tpu as pltpu
from jax.sharding import Mesh, PartitionSpec as P

HIGHEST = lax.Precision.HIGHEST
damping = 0.1


def dot_nn(a, b):
    return lax.dot_general(a, b, (((1,), (0,)), ((), ())), precision=HIGHEST, preferred_element_type=jnp.float32)


def dot_nt(a, b):
    return lax.dot_general(a, b, (((1,), (1,)), ((), ())), precision=HIGHEST, preferred_element_type=jnp.float32)


def dot_tn(a, b):
    return lax.dot_general(a, b, (((0,), (0,)), ((), ())), precision=HIGHEST, preferred_element_type=jnp.float32)


def reciprocal(p):
    r = pl.reciprocal(p, approx=True)
    r = r * (2.0 - p * r)
    return r * (2.0 - p * r)


def inverse_128(matrix):
    rows = [matrix[8 * r:8 * r + 8, :] for r in range(16)]
    lane = lax.broadcasted_iota(jnp.int32, (8, 128), 1)
    sub = lax.broadcasted_iota(jnp.int32, (8, 128), 0)
    spread = lambda x, l: jnp.broadcast_to(x[:, l:l + 1], (8, 128))
    row_of = lambda x, i: jnp.broadcast_to(x[i:i + 1, :], (8, 128))
    for kb in range(16):
        in_block = (lane >= 8 * kb) & (lane < 8 * kb + 8)
        unit = (lane - 8 * kb == sub).astype(jnp.float32)
        held = rows[kb]
        cols = [spread(held, 8 * kb + i) for i in range(8)]
        z = jnp.where(in_block, unit, held)
        for i in range(0, 8, 2):
            first, second = cols[i], cols[i + 1]
            a, b, c = row_of(first, i), row_of(second, i), row_of(second, i + 1)
            r = reciprocal(a * c - b * b)
            at_i, at_j = sub == i, sub == i + 1
            pivots = at_i | at_j
            m0 = jnp.where(at_i, -1.0, jnp.where(at_j, 0.0, first))
            m1 = jnp.where(at_j, -1.0, jnp.where(at_i, 0.0, second))
            f0 = (m0 * c - m1 * b) * r
            f1 = (m1 * a - m0 * b) * r
            step = lambda v: jnp.where(pivots, 0.0, v) - f0 * row_of(v, i) - f1 * row_of(v, i + 1)
            z = step(z)
            for j in range(i + 2, 8):
                cols[j] = step(cols[j])
        z = jnp.where(in_block, -z, z)
        z_rows = [row_of(z, i) for i in range(8)]
        order = [(kb + 1 + r) % 16 for r in range(15)]
        for r in order:
            old = rows[r]
            acc = jnp.where(in_block, 0.0, old)
            for i in range(8):
                acc = acc - spread(old, 8 * kb + i) * z_rows[i]
            rows[r] = acc
        rows[kb] = z
    return -jnp.concatenate(rows, axis=0)


def factor_kernel(n, scale, g_ref, l_ref, d_ref, a_ref):
    place = lambda i, j: j * n - j * (j - 1) // 2 + (i - j)
    blocks = n * (n + 1) // 2
    eye = (lax.broadcasted_iota(jnp.int32, (256, 256), 0) == lax.broadcasted_iota(jnp.int32, (256, 256), 1)).astype(jnp.float32)
    diagonal = [place(j, j) for j in range(n)]
    for k in range(blocks):
        block = jnp.concatenate([g_ref[2 * k], g_ref[2 * k + 1]], axis=1) * scale
        a_ref[k] = block + damping * eye if k in diagonal else block
    def column_step(j, _):
        p = j * n - (j * (j - 1)) // 2
        d = a_ref.at[p]
        d11 = d[0:128, 0:128]
        d21 = d[128:256, 0:128]
        d22 = d[128:256, 128:256]
        i11 = inverse_128(d11)
        x = dot_nn(d21, i11)
        i22 = inverse_128(d22 - dot_nt(x, d21))
        u = dot_nn(i22, x)
        d_ref[j, 0:128, 0:128] = i11 + dot_tn(x, u)
        d_ref[j, 128:256, 0:128] = -u
        d_ref[j, 0:128, 128:256] = -u.T
        d_ref[j, 128:256, 128:256] = i22
        def panel(i, _):
            q = p + i - j
            l_ref[q] = dot_nn(a_ref[q], d_ref[j])
            return 0
        lax.fori_loop(j + 1, n, panel, 0)
        def column(c, _):
            pc = c * n - (c * (c - 1)) // 2
            def block(i, _):
                a_ref[pc + i - c] = a_ref[pc + i - c] - dot_nt(l_ref[p + i - j], a_ref[p + c - j])
                return 0
            lax.fori_loop(c, n, block, 0)
            return 0
        lax.fori_loop(j + 1, n, column, 0)
        return 0
    lax.fori_loop(0, n, column_step, 0)


def factor(g, n, scale):
    blocks = n * (n + 1) // 2
    return pl.pallas_call(
        functools.partial(factor_kernel, n, scale),
        out_shape=(
            jax.ShapeDtypeStruct((blocks, 256, 256), jnp.float32),
            jax.ShapeDtypeStruct((n, 256, 256), jnp.float32),
        ),
        in_specs=[pl.BlockSpec(memory_space=pltpu.VMEM)],
        out_specs=(pl.BlockSpec(memory_space=pltpu.VMEM),) * 2,
        scratch_shapes=[pltpu.VMEM((blocks, 256, 256), jnp.float32)],
        compiler_params=pltpu.CompilerParams(vmem_limit_bytes=40 * 1024 * 1024),
    )(g)


def split(x):
    high = x.astype(jnp.bfloat16)
    return high, (x - high.astype(jnp.float32)).astype(jnp.bfloat16)


def dot3(a, b, dims):
    d = lambda u, v: lax.dot_general(u, v, (dims, ((), ())), preferred_element_type=jnp.float32)
    return d(a[0], b[1]) + d(a[1], b[0]) + d(a[0], b[0])


NN = ((1,), (0,))
NT = ((1,), (1,))


def score_kernel(n, scale, pick_ref, t_ref, l_ref, d_ref, v_ref, out_ref, wh_ref, wl_ref):
    step = pl.program_id(0)
    place = lambda i, j: j * n - j * (j - 1) // 2 + (i - j)

    @pl.when(step == 0)
    def _():
        ys = []
        for j in range(n):
            acc = t_ref[:, 256 * j:256 * j + 256]
            for i in range(j):
                acc = acc - dot3(ys[i], split(l_ref[place(j, i)]), NT)
            ys.append(split(acc))
        ws = [None] * n
        for j in reversed(range(n)):
            acc = dot3(ys[j], split(d_ref[j]), NN)
            for i in range(j + 1, n):
                acc = acc - dot3(ws[i], split(l_ref[place(i, j)]), NN)
            ws[j] = split(acc)
        for j in range(n):
            wh_ref[:, 256 * j:256 * j + 256] = ws[j][0] * jnp.bfloat16(scale)
            wl_ref[:, 256 * j:256 * j + 256] = ws[j][1] * jnp.bfloat16(scale)

    slots = v_ref.shape[0]
    rows = []
    for s in range(slots):
        pick = pick_ref[step * slots + s]
        first = (pick == 0).astype(jnp.float32)
        second = (pick == 1).astype(jnp.float32)
        for y in range(v_ref.shape[1]):
            rows.append(v_ref[s, y, 0] * first + v_ref[s, y, 1] * second)
    v = split(jnp.concatenate(rows, axis=0))
    out_ref[...] = dot3((wh_ref[...], wl_ref[...]), v, NT)


def score(pick, t, l, d, v, n, slots):
    m, features = t.shape
    total, groups, blocks, part, _ = v.shape
    width = slots * groups * part
    whole = pl.BlockSpec(memory_space=pltpu.VMEM)
    return pl.pallas_call(
        functools.partial(score_kernel, n, features ** -0.5),
        grid=(total // slots,),
        out_shape=jax.ShapeDtypeStruct((m, total * groups * part), jnp.float32),
        in_specs=[
            pl.BlockSpec(memory_space=pltpu.SMEM),
            whole, whole, whole,
            pl.BlockSpec((slots, groups, blocks, part, features), lambda i: (i, 0, 0, 0, 0)),
        ],
        out_specs=pl.BlockSpec((m, width), lambda i: (0, i)),
        scratch_shapes=[pltpu.VMEM((m, features), jnp.bfloat16)] * 2,
        compiler_params=pltpu.CompilerParams(vmem_limit_bytes=56 * 1024 * 1024),
    )(pick, t, l, d, v)


def gram_kernel(n, t_ref, g_ref, th_ref, tl_ref):
    for j in range(n):
        at = slice(256 * j, 256 * j + 256)
        high, low = split(t_ref[:, at])
        th_ref[at, :] = high.T
        tl_ref[at, :] = low.T
    k = 0
    for j in range(n):
        at = slice(256 * j, 256 * j + 256)
        right = split(t_ref[:, at])
        for i in range(j, n):
            of = slice(256 * i, 256 * i + 256)
            block = dot3((th_ref[of, :], tl_ref[of, :]), right, NN)
            g_ref[2 * k] = block[:, 0:128]
            g_ref[2 * k + 1] = block[:, 128:256]
            k += 1


def gram(t, n):
    m, features = t.shape
    return pl.pallas_call(
        functools.partial(gram_kernel, n),
        out_shape=jax.ShapeDtypeStruct((n * (n + 1), 256, 128), jnp.float32),
        in_specs=[pl.BlockSpec(memory_space=pltpu.VMEM)],
        out_specs=pl.BlockSpec(memory_space=pltpu.VMEM),
        scratch_shapes=[pltpu.VMEM((features, m), jnp.bfloat16)] * 2,
        compiler_params=pltpu.CompilerParams(vmem_limit_bytes=40 * 1024 * 1024),
    )(t)


def swap(v, axis):
    return lax.ppermute(v, axis, [(0, 1), (1, 0)])


def scatter_pair(v, axis):
    me = lax.axis_index(axis)
    mine = lax.dynamic_index_in_dim(v, me, 0, keepdims=False)
    other = lax.dynamic_index_in_dim(v, 1 - me, 0, keepdims=False)
    return mine + swap(other, axis)


def gather_pair(v, axis):
    me = lax.axis_index(axis)
    other = swap(v, axis)
    return jnp.stack([jnp.where(me == 0, v, other), jnp.where(me == 0, other, v)])


def scatter_ring(v, axis):
    size = lax.axis_size(axis)
    me = lax.axis_index(axis)
    part = lambda k: lax.dynamic_index_in_dim(v, lax.rem(me + k, size), 0, keepdims=False)
    total = part(0)
    for k in range(1, size):
        total = total + lax.ppermute(part(k), axis, [(i, (i + k) % size) for i in range(size)])
    return total


def gather_ring(v, axis):
    size = lax.axis_size(axis)
    me = lax.axis_index(axis)
    out = jnp.zeros((size,) + v.shape, v.dtype)
    out = lax.dynamic_update_index_in_dim(out, v, me, 0)
    for k in range(1, size):
        came = lax.ppermute(v, axis, [(i, (i + k) % size) for i in range(size)])
        out = lax.dynamic_update_index_in_dim(out, came, lax.rem(me + size - k, size), 0)
    return out


def scatter_direct(v, axis):
    return lax.all_to_all(v, axis, 0, 0, tiled=True).sum(0)


def gather_direct(v, axis):
    size = lax.axis_size(axis)
    return lax.all_to_all(jnp.broadcast_to(v[None], (size,) + v.shape), axis, 0, 0, tiled=True)


def sum_all(v):
    rows, lanes = v.shape
    v = scatter_pair(v.reshape(2, -1, lanes), "core")
    v = scatter_ring(v.reshape(lax.axis_size("y"), -1, lanes), "y")
    v = scatter_ring(v.reshape(lax.axis_size("x"), -1, lanes), "x")
    v = scatter_direct(v.reshape(lax.axis_size("z"), -1, lanes), "z")
    v = gather_direct(v, "z").reshape(-1, lanes)
    v = gather_ring(v, "x").reshape(-1, lanes)
    v = gather_ring(v, "y").reshape(-1, lanes)
    return gather_pair(v, "core").reshape(rows, lanes)


def local(train_grads, val_grads, wanted, owner):
    m, features = train_grads.shape
    n = features // 256
    dp = ("z", "x", "core")
    slabs, group = lax.axis_size(dp), lax.axis_size("y")
    blocks, part, _ = val_grads.shape
    val_all = lax.all_gather(val_grads, dp + ("y",), tiled=False)
    val_all = val_all.reshape(slabs, group, blocks, part, features)

    positions = jnp.arange(slabs, dtype=jnp.int32)
    holder = jnp.sum(jnp.where(owner == lax.axis_index(dp), positions, 0))
    request = lax.dynamic_index_in_dim(wanted, holder, 0, keepdims=False)
    pick = jnp.where(request >= 0, request - positions * blocks, -1)

    g = gram(train_grads, n)
    g = sum_all(g.reshape(-1, 128)).reshape(g.shape)
    l, d = factor(g, n, 1.0 / (m * slabs * group))
    return score(pick, train_grads, l, d, val_all, n, 8)


def solution(mesh):
    axes = ("z", "x", "core", "y")
    fine = Mesh(mesh.devices.reshape(8, 4, 2, 4), axes)
    dp = P(("z", "x", "core"), "y", None)
    in_specs = (P(axes, None), dp, P(), P())
    return jax.shard_map(local, mesh=fine, in_specs=in_specs, out_specs=P(axes, None), check_vma=False)
```

```python
import functools
import jax
import jax.numpy as jnp
from jax import lax
from jax.experimental import pallas as pl
from jax.experimental.pallas import tpu as pltpu
from jax.sharding import Mesh, PartitionSpec as P

HIGHEST = lax.Precision.HIGHEST
damping = 0.1
NN = ((1,), (0,))
NT = ((1,), (1,))
TN = ((0,), (0,))
MIB = 1024 * 1024


def dot(a, b, dims):
    return lax.dot_general(a, b, (dims, ((), ())), precision=HIGHEST, preferred_element_type=jnp.float32)


def split(x):
    high = x.astype(jnp.bfloat16)
    return high, (x - high.astype(jnp.float32)).astype(jnp.bfloat16)


def dot3(a, b, dims):
    d = lambda u, v: lax.dot_general(u, v, (dims, ((), ())), preferred_element_type=jnp.float32)
    return d(a[0], b[1]) + d(a[1], b[0]) + d(a[0], b[0])


def thirds(x):
    high = x.astype(jnp.bfloat16).astype(jnp.float32)
    rest = x - high
    middle = rest.astype(jnp.bfloat16).astype(jnp.float32)
    return high, middle, rest - middle


def inverse_128(matrix):
    width = 2
    pivots = 8 * width
    rows = [matrix[8 * r:8 * r + 8, :] for r in range(16)]
    lane = lax.broadcasted_iota(jnp.int32, (8, 128), 1)
    sub = lax.broadcasted_iota(jnp.int32, (8, 128), 0)
    spread = lambda x, l: jnp.broadcast_to(x[:, l:l + 1], (8, 128))
    row_of = lambda v, i: jnp.broadcast_to(v[i // 8][i % 8:i % 8 + 1, :], (8, 128))
    stack = lambda v: jnp.concatenate(v, axis=0)
    for lo in range(0, 128, pivots):
        first_row = lo // 8
        in_block = (lane >= lo) & (lane < lo + pivots)
        held = rows[first_row:first_row + width]
        cols = [[spread(h, lo + i) for h in held] for i in range(pivots)]
        z = [jnp.where(in_block, (lane - lo == sub + 8 * t).astype(jnp.float32), held[t]) for t in range(width)]
        for i in range(0, pivots, 2):
            one, two = cols[i], cols[i + 1]
            a, b, c = row_of(one, i), row_of(two, i), row_of(two, i + 1)
            r = pl.reciprocal(a * c - b * b)
            at = i // 8
            at_i, at_j = sub == i % 8, sub == i % 8 + 1
            both = at_i | at_j
            m0, m1 = list(one), list(two)
            m0[at] = jnp.where(at_i, -1.0, jnp.where(at_j, 0.0, one[at]))
            m1[at] = jnp.where(at_j, -1.0, jnp.where(at_i, 0.0, two[at]))
            e0 = [x * c - y * b for x, y in zip(m0, m1)]
            e1 = [y * a - x * b for x, y in zip(m0, m1)]

            def step(v):
                ri, rj = row_of(v, i) * r, row_of(v, i + 1) * r
                kept = [jnp.where(both, 0.0, v[t]) if t == at else v[t] for t in range(width)]
                return [kept[t] - (e0[t] * ri + e1[t] * rj) for t in range(width)]

            z = step(z)
            for j in range(i + 2, pivots):
                cols[j] = step(cols[j])
        z = [jnp.where(in_block, -v, v) for v in z]
        z_rows = [row_of(z, i) for i in range(pivots)]
        order = [(first_row + width + r) % 16 for r in range(16 - width)]
        for r in order[:width]:
            terms = [spread(rows[r], lo + i) * z_rows[i] for i in range(pivots)]
            while len(terms) > 1:
                terms = [terms[2 * t] + terms[2 * t + 1] for t in range(len(terms) // 2)]
            rows[r] = jnp.where(in_block, 0.0, rows[r]) - terms[0]
        h, m, l = thirds(stack(held))
        zh, zm, zl = thirds(stack(z))
        left = stack([h, h, m, m, h, l]).astype(jnp.bfloat16)
        right = stack([zh, zm, zh, zm, zl, zh]).astype(jnp.bfloat16)
        change = lax.dot_general(left, right, (TN, ((), ())), preferred_element_type=jnp.float32)
        for r in order[width:]:
            rows[r] = jnp.where(in_block, 0.0, rows[r]) - change[8 * r:8 * r + 8]
        rows[first_row:first_row + width] = z
    return -stack(rows)


def small_blocks(n):
    out, place = [], 0
    for j in range(n):
        for i in range(j, n):
            out += [(place, 0, 0), (place, 128, 0)] + ([(place, 0, 128)] if i > j else []) + [(place, 128, 128)]
            place += 1
    return out


def gram_kernel(n, core_ref, t_ref, mine_ref, other_ref, th_ref, tl_ref):
    core = core_ref[0]
    for j in range(n):
        at = slice(256 * j, 256 * j + 256)
        high, low = split(t_ref[:, at])
        th_ref[at, :] = high.T
        tl_ref[at, :] = low.T
    list_of = small_blocks(n)
    half = len(list_of) // 2
    place = 0
    for j in range(n):
        right = split(t_ref[:, 256 * j:256 * j + 256])
        for i in range(j, n):
            of = slice(256 * i, 256 * i + 256)
            block = dot3((th_ref[of, :], tl_ref[of, :]), right, NN)
            for k, (p, row, column) in enumerate(list_of):
                if p == place:
                    part = block[row:row + 128, column:column + 128]
                    at = k % half

                    @pl.when(core == k // half)
                    def _():
                        mine_ref[at] = part

                    @pl.when(core != k // half)
                    def _():
                        other_ref[at] = part
            place += 1


def gram(core, t, n):
    m, features = t.shape
    half = len(small_blocks(n)) // 2
    whole = pl.BlockSpec(memory_space=pltpu.VMEM)
    return pl.pallas_call(
        functools.partial(gram_kernel, n),
        out_shape=(jax.ShapeDtypeStruct((half, 128, 128), jnp.float32),) * 2,
        in_specs=[pl.BlockSpec(memory_space=pltpu.SMEM), whole],
        out_specs=(whole,) * 2,
        scratch_shapes=[pltpu.VMEM((features, m), jnp.bfloat16)] * 2,
        compiler_params=pltpu.CompilerParams(vmem_limit_bytes=28 * MIB),
    )(core, t)


def factor_kernel(n, scale, core_ref, mine_ref, other_ref, l_ref, d_ref, a_ref):
    core = core_ref[0]
    list_of = small_blocks(n)
    half = len(list_of) // 2
    eye = lax.broadcasted_iota(jnp.int32, (128, 128), 0) == lax.broadcasted_iota(jnp.int32, (128, 128), 1)
    damp = damping * eye.astype(jnp.float32)
    diagonal = [j * n - j * (j - 1) // 2 for j in range(n)]
    for k, (p, row, column) in enumerate(list_of):
        block = jnp.where(core == k // half, mine_ref[k % half], other_ref[k % half]) * scale
        a_ref[p, row:row + 128, column:column + 128] = block + damp if p in diagonal and row == column else block

    def column_step(j, _):
        p = j * n - (j * (j - 1)) // 2
        d = a_ref.at[p]
        d21 = d[128:256, 0:128]
        i11 = inverse_128(d[0:128, 0:128])
        x = dot(d21, i11, NN)
        i22 = inverse_128(d[128:256, 128:256] - dot(x, d21, NT))
        u = dot(i22, x, NN)
        d_ref[j, 0:128, 0:128] = i11 + dot(x, u, TN)
        d_ref[j, 128:256, 0:128] = -u
        d_ref[j, 0:128, 128:256] = -u.T
        d_ref[j, 128:256, 128:256] = i22

        def row_step(i, _):
            panel = dot(a_ref[p + i - j], d_ref[j], NN)
            l_ref[p + i - j] = panel

            def block_step(c, _):
                q = c * n - (c * (c - 1)) // 2 + i - c
                a_ref[q] = a_ref[q] - dot(panel, a_ref[p + c - j], NT)
                return 0

            lax.fori_loop(j + 1, i + 1, block_step, 0)
            return 0

        lax.fori_loop(j + 1, n, row_step, 0)
        return 0

    lax.fori_loop(0, n, column_step, 0)


def factor(core, mine, other, n, scale):
    blocks = n * (n + 1) // 2
    whole = pl.BlockSpec(memory_space=pltpu.VMEM)
    return pl.pallas_call(
        functools.partial(factor_kernel, n, scale),
        out_shape=(
            jax.ShapeDtypeStruct((blocks, 256, 256), jnp.float32),
            jax.ShapeDtypeStruct((n, 256, 256), jnp.float32),
        ),
        in_specs=[pl.BlockSpec(memory_space=pltpu.SMEM), whole, whole],
        out_specs=(whole,) * 2,
        scratch_shapes=[pltpu.VMEM((blocks, 256, 256), jnp.float32)],
        compiler_params=pltpu.CompilerParams(vmem_limit_bytes=20 * MIB),
    )(core, mine, other)


def solve_kernel(n, scale, t_ref, l_ref, d_ref, wh_ref, wl_ref):
    place = lambda i, j: j * n - j * (j - 1) // 2 + (i - j)
    at = lambda j: slice(256 * j, 256 * j + 256)
    ys = []
    for j in range(n):
        acc = t_ref[:, at(j)]
        for i in range(j):
            acc = acc - dot3(ys[i], split(l_ref[place(j, i)]), NT)
        ys.append(split(acc))
    ws = [None] * n
    for j in reversed(range(n)):
        acc = dot3(ys[j], split(d_ref[j]), NN)
        for i in range(j + 1, n):
            acc = acc - dot3(ws[i], split(l_ref[place(i, j)]), NN)
        ws[j] = split(acc)
        wh_ref[:, at(j)] = ws[j][0] * jnp.bfloat16(scale)
        wl_ref[:, at(j)] = ws[j][1] * jnp.bfloat16(scale)


def solve(t, l, d, n):
    m, features = t.shape
    whole = pl.BlockSpec(memory_space=pltpu.VMEM)
    return pl.pallas_call(
        functools.partial(solve_kernel, n, features ** -0.5),
        out_shape=(jax.ShapeDtypeStruct((m, features), jnp.bfloat16),) * 2,
        in_specs=[whole] * 3,
        out_specs=(whole,) * 2,
        compiler_params=pltpu.CompilerParams(vmem_limit_bytes=36 * MIB),
    )(t, l, d)


def score_kernel(pick_ref, wh_ref, wl_ref, v_ref, out_ref):
    step = pl.program_id(0)
    slots = v_ref.shape[0]
    rows = []
    for s in range(slots):
        pick = pick_ref[step * slots + s]
        first = (pick == 0).astype(jnp.float32)
        second = (pick == 1).astype(jnp.float32)
        for y in range(v_ref.shape[1]):
            rows.append(v_ref[s, y, 0] * first + v_ref[s, y, 1] * second)
    v = split(jnp.concatenate(rows, axis=0))
    out_ref[...] = dot3((wh_ref[...], wl_ref[...]), v, NT)


def score(pick, wh, wl, v, slots):
    m, features = wh.shape
    total, groups, blocks, part, _ = v.shape
    width = slots * groups * part
    whole = pl.BlockSpec(memory_space=pltpu.VMEM)
    return pl.pallas_call(
        score_kernel,
        grid=(total // slots,),
        out_shape=jax.ShapeDtypeStruct((m, total * groups * part), jnp.float32),
        in_specs=[
            pl.BlockSpec(memory_space=pltpu.SMEM),
            whole, whole,
            pl.BlockSpec((slots, groups, blocks, part, features), lambda i: (i, 0, 0, 0, 0)),
        ],
        out_specs=pl.BlockSpec((m, width), lambda i: (0, i)),
        compiler_params=pltpu.CompilerParams(vmem_limit_bytes=32 * MIB),
    )(pick, wh, wl, v)


def swap(v):
    return lax.ppermute(v, "core", [(0, 1), (1, 0)])


def ring(v, axis, k):
    size = lax.axis_size(axis)
    return lax.ppermute(v, axis, [(i, (i + k) % size) for i in range(size)])


def scatter(v, axis, dim):
    size, me = lax.axis_size(axis), lax.axis_index(axis)
    part = lambda k: lax.dynamic_index_in_dim(v, lax.rem(me + k, size), dim, keepdims=False)
    came = [ring(part(k), axis, k) for k in range(1, size)]
    return part(0), came


def gather(v, axis):
    size, me = lax.axis_size(axis), lax.axis_index(axis)
    came = [ring(v, axis, k) for k in range(1, size)]
    out = lax.dynamic_update_index_in_dim(jnp.zeros((size,) + v.shape, v.dtype), v, me, 0)
    for k in range(1, size):
        out = lax.dynamic_update_index_in_dim(out, came[k - 1], lax.rem(me + size - k, size), 0)
    return out


def add(parts):
    total = parts[0]
    for c in parts[1]:
        total = total + c
    return total


def sum_all(mine, other, beside):
    shape = mine.shape
    ny, nx, nz = lax.axis_size("y"), lax.axis_size("x"), lax.axis_size("z")
    v = (mine + swap(other)).reshape(ny, nx, 2, -1, 128)
    by_y, by_x = scatter(v[:, :, 0], "y", 0), scatter(v[:, :, 1], "x", 1)
    left, right = add(by_y), add(by_x)
    left, beside = lax.optimization_barrier((left, beside))
    by_x, by_y = scatter(left, "x", 0), scatter(right, "y", 0)
    s = jnp.stack([add(by_x), add(by_y)])
    hop = 1
    while hop < nz:
        s = s + lax.ppermute(s, "z", [(i, i ^ hop) for i in range(nz)])
        hop *= 2
    return gather(gather(s, "x"), "y").reshape(shape), beside


def local(train_grads, val_grads, wanted, owner):
    m, features = train_grads.shape
    n = features // 256
    dp = ("z", "x", "core")
    slabs, group = lax.axis_size(dp), lax.axis_size("y")
    blocks, part, _ = val_grads.shape
    val_all = lax.all_gather(val_grads, dp + ("y",), tiled=False)
    val_all = val_all.reshape(slabs, group, blocks, part, features)

    positions = jnp.arange(slabs, dtype=jnp.int32)
    holder = jnp.sum(jnp.where(owner == lax.axis_index(dp), positions, 0))
    request = lax.dynamic_index_in_dim(wanted, holder, 0, keepdims=False)
    pick = jnp.where(request >= 0, request - positions * blocks, -1)

    core = lax.axis_index("core").reshape(1)
    mine, other = gram(core, train_grads, n)
    mine, pick = sum_all(mine, other, pick)
    l, d = factor(core, mine, swap(mine), n, 1.0 / (m * slabs * group))
    wh, wl = solve(train_grads, l, d, n)
    return score(pick, wh, wl, val_all, 8)


def solution(mesh):
    axes = ("z", "x", "core", "y")
    fine = Mesh(mesh.devices.reshape(8, 4, 2, 4), axes)
    dp = P(("z", "x", "core"), "y", None)
    in_specs = (P(axes, None), dp, P(), P())
    return jax.shard_map(local, mesh=fine, in_specs=in_specs, out_specs=P(axes, None), check_vma=False)
```

```python
import functools
import jax
import jax.numpy as jnp
from jax import lax
from jax.experimental import pallas as pl
from jax.experimental.pallas import tpu as pltpu
from jax.sharding import Mesh, PartitionSpec as P

HIGHEST = lax.Precision.HIGHEST
damping = 0.1
NN = ((1,), (0,))
NT = ((1,), (1,))
TN = ((0,), (0,))
MIB = 1024 * 1024


def cost(flops, size):
    return pl.CostEstimate(flops=flops, bytes_accessed=size, transcendentals=0)


def dot(a, b, dims):
    return lax.dot_general(a, b, (dims, ((), ())), precision=HIGHEST, preferred_element_type=jnp.float32)


def split(x):
    high = x.astype(jnp.bfloat16)
    return high, (x - high.astype(jnp.float32)).astype(jnp.bfloat16)


def dot3(a, b, dims):
    d = lambda u, v: lax.dot_general(u, v, (dims, ((), ())), preferred_element_type=jnp.float32)
    return d(a[0], b[1]) + d(a[1], b[0]) + d(a[0], b[0])


def thirds(x):
    high = x.astype(jnp.bfloat16).astype(jnp.float32)
    rest = x - high
    middle = rest.astype(jnp.bfloat16).astype(jnp.float32)
    return high, middle, rest - middle


def inverse_128(matrix):
    width = 2
    pivots = 8 * width
    rows = [matrix[8 * r:8 * r + 8, :] for r in range(16)]
    lane = lax.broadcasted_iota(jnp.int32, (8, 128), 1)
    sub = lax.broadcasted_iota(jnp.int32, (8, 128), 0)
    spread = lambda x, l: jnp.broadcast_to(x[:, l:l + 1], (8, 128))
    row_of = lambda v, i: jnp.broadcast_to(v[i // 8][i % 8:i % 8 + 1, :], (8, 128))
    stack = lambda v: jnp.concatenate(v, axis=0)
    for lo in range(0, 128, pivots):
        first_row = lo // 8
        in_block = (lane >= lo) & (lane < lo + pivots)
        held = rows[first_row:first_row + width]
        cols = [[spread(h, lo + i) for h in held] for i in range(pivots)]
        z = [jnp.where(in_block, (lane - lo == sub + 8 * t).astype(jnp.float32), held[t]) for t in range(width)]
        for i in range(0, pivots, 2):
            one, two = cols[i], cols[i + 1]
            a, b, c = row_of(one, i), row_of(two, i), row_of(two, i + 1)
            r = pl.reciprocal(a * c - b * b)
            at = i // 8
            at_i, at_j = sub == i % 8, sub == i % 8 + 1
            both = at_i | at_j
            m0, m1 = list(one), list(two)
            m0[at] = jnp.where(at_i, -1.0, jnp.where(at_j, 0.0, one[at]))
            m1[at] = jnp.where(at_j, -1.0, jnp.where(at_i, 0.0, two[at]))
            e0 = [x * c - y * b for x, y in zip(m0, m1)]
            e1 = [y * a - x * b for x, y in zip(m0, m1)]

            def step(v):
                ri, rj = row_of(v, i) * r, row_of(v, i + 1) * r
                kept = [jnp.where(both, 0.0, v[t]) if t == at else v[t] for t in range(width)]
                return [kept[t] - (e0[t] * ri + e1[t] * rj) for t in range(width)]

            z = step(z)
            for j in range(i + 2, pivots):
                cols[j] = step(cols[j])
        z = [jnp.where(in_block, -v, v) for v in z]
        z_rows = [row_of(z, i) for i in range(pivots)]
        order = [(first_row + width + r) % 16 for r in range(16 - width)]
        for r in order[:width]:
            terms = [spread(rows[r], lo + i) * z_rows[i] for i in range(pivots)]
            while len(terms) > 1:
                terms = [terms[2 * t] + terms[2 * t + 1] for t in range(len(terms) // 2)]
            rows[r] = jnp.where(in_block, 0.0, rows[r]) - terms[0]
        h, m, l = thirds(stack(held))
        zh, zm, zl = thirds(stack(z))
        left = stack([h, h, m, m, h, l]).astype(jnp.bfloat16)
        right = stack([zh, zm, zh, zm, zl, zh]).astype(jnp.bfloat16)
        change = lax.dot_general(left, right, (TN, ((), ())), preferred_element_type=jnp.float32)
        for r in order[width:]:
            rows[r] = jnp.where(in_block, 0.0, rows[r]) - change[8 * r:8 * r + 8]
        rows[first_row:first_row + width] = z
    return -stack(rows)


def small_blocks(n):
    out, place = [], 0
    for j in range(n):
        for i in range(j, n):
            out += [(place, 0, 0), (place, 128, 0)] + ([(place, 0, 128)] if i > j else []) + [(place, 128, 128)]
            place += 1
    return out


def gram_kernel(n, core_ref, t_ref, mine_ref, other_ref, th_ref, tl_ref, halves_ref):
    core = core_ref[0]
    for j in range(n):
        at = slice(256 * j, 256 * j + 256)
        high, low = split(t_ref[:, at])
        th_ref[at, :] = high.T
        tl_ref[at, :] = low.T
    list_of = small_blocks(n)
    half = len(list_of) // 2
    place = 0
    for j in range(n):
        right = split(t_ref[:, 256 * j:256 * j + 256])
        for i in range(j, n):
            of = slice(256 * i, 256 * i + 256)
            block = dot3((th_ref[of, :], tl_ref[of, :]), right, NN)
            for k, (p, row, column) in enumerate(list_of):
                if p == place:
                    halves_ref[core ^ (k // half), k % half] = block[row:row + 128, column:column + 128]
            place += 1
    mine_ref[...] = halves_ref[0]
    other_ref[...] = halves_ref[1]


def gram(core, t, n):
    m, features = t.shape
    half = len(small_blocks(n)) // 2
    whole = pl.BlockSpec(memory_space=pltpu.VMEM)
    return pl.pallas_call(
        functools.partial(gram_kernel, n),
        out_shape=(jax.ShapeDtypeStruct((half, 128, 128), jnp.float32),) * 2,
        in_specs=[pl.BlockSpec(memory_space=pltpu.SMEM), whole],
        out_specs=(whole,) * 2,
        scratch_shapes=[pltpu.VMEM((features, m), jnp.bfloat16)] * 2 + [pltpu.VMEM((2, half, 128, 128), jnp.float32)],
        compiler_params=pltpu.CompilerParams(vmem_limit_bytes=28 * MIB),
        cost_estimate=cost(6 * m * features * features, 7 * MIB),
    )(core, t)


def factor_kernel(n, scale, core_ref, mine_ref, other_ref, l_ref, d_ref, a_ref):
    core = core_ref[0]
    list_of = small_blocks(n)
    half = len(list_of) // 2
    eye = lax.broadcasted_iota(jnp.int32, (128, 128), 0) == lax.broadcasted_iota(jnp.int32, (128, 128), 1)
    damp = damping * eye.astype(jnp.float32)
    diagonal = [j * n - j * (j - 1) // 2 for j in range(n)]
    for k, (p, row, column) in enumerate(list_of):
        block = jnp.where(core == k // half, mine_ref[k % half], other_ref[k % half]) * scale
        a_ref[p, row:row + 128, column:column + 128] = block + damp if p in diagonal and row == column else block

    def column_step(j, _):
        p = j * n - (j * (j - 1)) // 2
        d = a_ref.at[p]
        d21 = d[128:256, 0:128]
        i11 = inverse_128(d[0:128, 0:128])
        x = dot(d21, i11, NN)
        i22 = inverse_128(d[128:256, 128:256] - dot(x, d21, NT))
        u = dot(i22, x, NN)
        d_ref[j, 0:128, 0:128] = i11 + dot(x, u, TN)
        d_ref[j, 128:256, 0:128] = -u
        d_ref[j, 0:128, 128:256] = -u.T
        d_ref[j, 128:256, 128:256] = i22

        def row_step(i, _):
            panel = dot(a_ref[p + i - j], d_ref[j], NN)
            l_ref[p + i - j] = panel

            def block_step(c, _):
                q = c * n - (c * (c - 1)) // 2 + i - c
                a_ref[q] = a_ref[q] - dot(panel, a_ref[p + c - j], NT)
                return 0

            lax.fori_loop(j + 1, i + 1, block_step, 0)
            return 0

        lax.fori_loop(j + 1, n, row_step, 0)
        return 0

    lax.fori_loop(0, n, column_step, 0)


def factor(core, mine, other, n, scale):
    blocks = n * (n + 1) // 2
    whole = pl.BlockSpec(memory_space=pltpu.VMEM)
    return pl.pallas_call(
        functools.partial(factor_kernel, n, scale),
        out_shape=(
            jax.ShapeDtypeStruct((blocks, 256, 256), jnp.float32),
            jax.ShapeDtypeStruct((n, 256, 256), jnp.float32),
        ),
        in_specs=[pl.BlockSpec(memory_space=pltpu.SMEM), whole, whole],
        out_specs=(whole,) * 2,
        scratch_shapes=[pltpu.VMEM((blocks, 256, 256), jnp.float32)],
        compiler_params=pltpu.CompilerParams(vmem_limit_bytes=20 * MIB),
        cost_estimate=cost(32 * (256 * n) ** 3, 6 * MIB),
    )(core, mine, other)


def solve_kernel(n, scale, t_ref, l_ref, d_ref, wh_ref, wl_ref):
    place = lambda i, j: j * n - j * (j - 1) // 2 + (i - j)
    at = lambda j: slice(256 * j, 256 * j + 256)
    ys = []
    for j in range(n):
        acc = t_ref[:, at(j)]
        for i in range(j):
            acc = acc - dot3(ys[i], split(l_ref[place(j, i)]), NT)
        ys.append(split(acc))
    ws = [None] * n
    for j in reversed(range(n)):
        acc = dot3(ys[j], split(d_ref[j]), NN)
        for i in range(j + 1, n):
            acc = acc - dot3(ws[i], split(l_ref[place(i, j)]), NN)
        ws[j] = split(acc)
        wh_ref[:, at(j)] = ws[j][0] * jnp.bfloat16(scale)
        wl_ref[:, at(j)] = ws[j][1] * jnp.bfloat16(scale)


def solve(t, l, d, n):
    m, features = t.shape
    whole = pl.BlockSpec(memory_space=pltpu.VMEM)
    return pl.pallas_call(
        functools.partial(solve_kernel, n, features ** -0.5),
        out_shape=(jax.ShapeDtypeStruct((m, features), jnp.bfloat16),) * 2,
        in_specs=[whole] * 3,
        out_specs=(whole,) * 2,
        compiler_params=pltpu.CompilerParams(vmem_limit_bytes=36 * MIB),
        cost_estimate=cost(6 * m * features * features, 12 * MIB),
    )(t, l, d)


def score_kernel(slots, pick_ref, wh_ref, wl_ref, *refs):
    step = pl.program_id(0)
    rows = []
    for s in range(slots):
        live = (pick_ref[step * slots + s] >= 0).astype(jnp.float32)
        block = refs[s][...]
        rows.append(block.reshape(-1, block.shape[-1]) * live)
    v = split(jnp.concatenate(rows, axis=0))
    refs[slots][...] = dot3((wh_ref[...], wl_ref[...]), v, NT)


def score(pick, wh, wl, v, slots):
    m, features = wh.shape
    total, groups, part = pick.shape[0], v.shape[1], v.shape[3]
    width = slots * groups * part
    whole = pl.BlockSpec(memory_space=pltpu.VMEM)

    def slot(s):
        def index(i, pick_ref):
            j = i * slots + s
            return lax.rem(j, v.shape[0]), 0, jnp.maximum(pick_ref[j], 0), 0, 0
        return pl.BlockSpec((1, groups, 1, part, features), index)

    return pl.pallas_call(
        functools.partial(score_kernel, slots),
        grid_spec=pltpu.PrefetchScalarGridSpec(
            num_scalar_prefetch=1,
            grid=(total // slots,),
            in_specs=[whole, whole] + [slot(s) for s in range(slots)],
            out_specs=pl.BlockSpec((m, width), lambda i, pick_ref: (0, i)),
        ),
        out_shape=jax.ShapeDtypeStruct((m, total * groups * part), jnp.float32),
        compiler_params=pltpu.CompilerParams(vmem_limit_bytes=48 * MIB),
        cost_estimate=cost(6 * m * width * total // slots * features, 20 * MIB),
    )(pick, wh, wl, *([v] * slots))


def swap(v):
    return lax.ppermute(v, "core", [(0, 1), (1, 0)])


def ring(v, axis, k):
    size = lax.axis_size(axis)
    return lax.ppermute(v, axis, [(i, (i + k) % size) for i in range(size)])


def scatter(v, axis, dim):
    size, me = lax.axis_size(axis), lax.axis_index(axis)
    part = lambda k: lax.dynamic_index_in_dim(v, lax.rem(me + k, size), dim, keepdims=False)
    came = [ring(part(k), axis, k) for k in range(1, size)]
    return part(0), came


def gather(v, axis):
    size, me = lax.axis_size(axis), lax.axis_index(axis)
    came = [ring(v, axis, k) for k in range(1, size)]
    out = lax.dynamic_update_index_in_dim(jnp.zeros((size,) + v.shape, v.dtype), v, me, 0)
    for k in range(1, size):
        out = lax.dynamic_update_index_in_dim(out, came[k - 1], lax.rem(me + size - k, size), 0)
    return out


def add(parts):
    total = parts[0]
    for c in parts[1]:
        total = total + c
    return total


def sum_all(mine, other, beside):
    shape = mine.shape
    ny, nx, nz = lax.axis_size("y"), lax.axis_size("x"), lax.axis_size("z")
    v = (mine + swap(other)).reshape(ny, nx, 2, -1, 128)
    by_y, by_x = scatter(v[:, :, 0], "y", 0), scatter(v[:, :, 1], "x", 1)
    left, right = add(by_y), add(by_x)
    left, right, beside = lax.optimization_barrier((left, right, beside))
    by_x, by_y = scatter(left, "x", 0), scatter(right, "y", 0)
    s = jnp.stack([add(by_x), add(by_y)])
    hop = 1
    while hop < nz:
        s = s + lax.ppermute(s, "z", [(i, i ^ hop) for i in range(nz)])
        hop *= 2
    return gather(gather(s, "x"), "y").reshape(shape), beside


def beside_z(v, hops):
    size = lax.axis_size("z")
    return jnp.concatenate([v] + [lax.ppermute(v, "z", [(i, i ^ h) for i in range(size)]) for h in hops])


def local(train_grads, val_grads, wanted, owner):
    m, features = train_grads.shape
    n = features // 256
    dp = ("z", "x", "core")
    slabs, group = lax.axis_size(dp), lax.axis_size("y")
    blocks, part, _ = val_grads.shape
    size = lax.axis_size("z")
    held = beside_z(val_grads, range(2, size, 2))

    positions = jnp.arange(slabs, dtype=jnp.int32)
    holder = jnp.sum(jnp.where(owner == lax.axis_index(dp), positions, 0))
    request = lax.dynamic_index_in_dim(wanted, holder, 0, keepdims=False)
    plane = slabs // size
    apart = (positions // plane) ^ lax.axis_index("z")
    at = (apart & 1) * (size // 2) + (apart >> 1)
    pick = jnp.where(request >= 0, at * blocks + request - positions * blocks, -1)

    core = lax.axis_index("core").reshape(1)
    mine, other = gram(core, train_grads, n)
    mine, other, held = lax.optimization_barrier((mine, other, held))
    mine, (pick, held) = sum_all(mine, other, (pick, beside_z(held, [1])))
    val_all = lax.all_gather(held, ("x", "core", "y"), tiled=False)
    val_all = val_all.reshape(plane, group, size * blocks, part, features)
    l, d = factor(core, mine, swap(mine), n, 1.0 / (m * slabs * group))
    wh, wl = solve(train_grads, l, d, n)
    return score(pick, wh, wl, val_all, 16)


def solution(mesh):
    axes = ("z", "x", "core", "y")
    fine = Mesh(mesh.devices.reshape(8, 4, 2, 4), axes)
    dp = P(("z", "x", "core"), "y", None)
    in_specs = (P(axes, None), dp, P(), P())
    return jax.shard_map(local, mesh=fine, in_specs=in_specs, out_specs=P(axes, None), check_vma=False)
```

```python
import functools
import jax
import jax.numpy as jnp
from jax import lax
from jax.experimental import pallas as pl
from jax.experimental.pallas import tpu as pltpu
from jax.sharding import Mesh, PartitionSpec as P

HIGHEST = lax.Precision.HIGHEST
damping = 0.1
NN = ((1,), (0,))
NT = ((1,), (1,))
TN = ((0,), (0,))
MIB = 1024 * 1024
Z = ("z_high", "z_low")


def cost(flops, size):
    return pl.CostEstimate(flops=flops, bytes_accessed=size, transcendentals=0)


def dot(a, b, dims):
    return lax.dot_general(a, b, (dims, ((), ())), precision=HIGHEST, preferred_element_type=jnp.float32)


def split(x):
    high = x.astype(jnp.bfloat16)
    return high, (x - high.astype(jnp.float32)).astype(jnp.bfloat16)


def dot3(a, b, dims):
    d = lambda u, v: lax.dot_general(u, v, (dims, ((), ())), preferred_element_type=jnp.float32)
    return d(a[0], b[1]) + d(a[1], b[0]) + d(a[0], b[0])


def thirds(x):
    high = x.astype(jnp.bfloat16).astype(jnp.float32)
    rest = x - high
    middle = rest.astype(jnp.bfloat16).astype(jnp.float32)
    return high, middle, rest - middle


def inverse_128(matrix):
    width = 2
    pivots = 8 * width
    rows = [matrix[8 * r:8 * r + 8, :] for r in range(16)]
    lane = lax.broadcasted_iota(jnp.int32, (8, 128), 1)
    sub = lax.broadcasted_iota(jnp.int32, (8, 128), 0)
    spread = lambda x, l: jnp.broadcast_to(x[:, l:l + 1], (8, 128))
    row_of = lambda v, i: jnp.broadcast_to(v[i // 8][i % 8:i % 8 + 1, :], (8, 128))
    stack = lambda v: jnp.concatenate(v, axis=0)
    for lo in range(0, 128, pivots):
        first_row = lo // 8
        in_block = (lane >= lo) & (lane < lo + pivots)
        held = rows[first_row:first_row + width]
        cols = [[spread(h, lo + i) for h in held] for i in range(pivots)]
        z = [jnp.where(in_block, (lane - lo == sub + 8 * t).astype(jnp.float32), held[t]) for t in range(width)]
        for i in range(0, pivots, 2):
            one, two = cols[i], cols[i + 1]
            a, b, c = row_of(one, i), row_of(two, i), row_of(two, i + 1)
            r = pl.reciprocal(a * c - b * b)
            at = i // 8
            at_i, at_j = sub == i % 8, sub == i % 8 + 1
            both = at_i | at_j
            m0, m1 = list(one), list(two)
            m0[at] = jnp.where(at_i, -1.0, jnp.where(at_j, 0.0, one[at]))
            m1[at] = jnp.where(at_j, -1.0, jnp.where(at_i, 0.0, two[at]))
            e0 = [x * c - y * b for x, y in zip(m0, m1)]
            e1 = [y * a - x * b for x, y in zip(m0, m1)]

            def step(v):
                ri, rj = row_of(v, i) * r, row_of(v, i + 1) * r
                kept = [jnp.where(both, 0.0, v[t]) if t == at else v[t] for t in range(width)]
                return [kept[t] - (e0[t] * ri + e1[t] * rj) for t in range(width)]

            z = step(z)
            for j in range(i + 2, pivots):
                cols[j] = step(cols[j])
        z = [jnp.where(in_block, -v, v) for v in z]
        z_rows = [row_of(z, i) for i in range(pivots)]
        order = [(first_row + width + r) % 16 for r in range(16 - width)]
        for r in order[:width]:
            terms = [spread(rows[r], lo + i) * z_rows[i] for i in range(pivots)]
            while len(terms) > 1:
                terms = [terms[2 * t] + terms[2 * t + 1] for t in range(len(terms) // 2)]
            rows[r] = jnp.where(in_block, 0.0, rows[r]) - terms[0]
        h, m, l = thirds(stack(held))
        zh, zm, zl = thirds(stack(z))
        left = stack([h, h, m, m, h, l]).astype(jnp.bfloat16)
        right = stack([zh, zm, zh, zm, zl, zh]).astype(jnp.bfloat16)
        change = lax.dot_general(left, right, (TN, ((), ())), preferred_element_type=jnp.float32)
        for r in order[width:]:
            rows[r] = jnp.where(in_block, 0.0, rows[r]) - change[8 * r:8 * r + 8]
        rows[first_row:first_row + width] = z
    return -stack(rows)


def small_blocks(n):
    out, place = [], 0
    for j in range(n):
        for i in range(j, n):
            out += [(place, 0, 0), (place, 128, 0)] + ([(place, 0, 128)] if i > j else []) + [(place, 128, 128)]
            place += 1
    return out


def gram_kernel(n, core_ref, t_ref, mine_ref, other_ref, th_ref, tl_ref, halves_ref):
    core = core_ref[0]
    for j in range(n):
        at = slice(256 * j, 256 * j + 256)
        high, low = split(t_ref[:, at])
        th_ref[at, :] = high.T
        tl_ref[at, :] = low.T
    list_of = small_blocks(n)
    half = len(list_of) // 2
    place = 0
    for j in range(n):
        right = split(t_ref[:, 256 * j:256 * j + 256])
        for i in range(j, n):
            of = slice(256 * i, 256 * i + 256)
            block = dot3((th_ref[of, :], tl_ref[of, :]), right, NN)
            for k, (p, row, column) in enumerate(list_of):
                if p == place:
                    halves_ref[core ^ (k // half), k % half] = block[row:row + 128, column:column + 128]
            place += 1
    mine_ref[...] = halves_ref[0]
    other_ref[...] = halves_ref[1]


def gram(core, t, n):
    m, features = t.shape
    half = len(small_blocks(n)) // 2
    whole = pl.BlockSpec(memory_space=pltpu.VMEM)
    return pl.pallas_call(
        functools.partial(gram_kernel, n),
        out_shape=(jax.ShapeDtypeStruct((half, 128, 128), jnp.float32),) * 2,
        in_specs=[pl.BlockSpec(memory_space=pltpu.SMEM), whole],
        out_specs=(whole,) * 2,
        scratch_shapes=[pltpu.VMEM((features, m), jnp.bfloat16)] * 2 + [pltpu.VMEM((2, half, 128, 128), jnp.float32)],
        compiler_params=pltpu.CompilerParams(vmem_limit_bytes=28 * MIB),
        cost_estimate=cost(6 * m * features * features, 7 * MIB),
    )(core, t)


def factor_kernel(n, scale, core_ref, mine_ref, other_ref, l_ref, d_ref, a_ref):
    core = core_ref[0]
    list_of = small_blocks(n)
    half = len(list_of) // 2
    eye = lax.broadcasted_iota(jnp.int32, (128, 128), 0) == lax.broadcasted_iota(jnp.int32, (128, 128), 1)
    damp = damping * eye.astype(jnp.float32)
    diagonal = [j * n - j * (j - 1) // 2 for j in range(n)]
    for k, (p, row, column) in enumerate(list_of):
        block = jnp.where(core == k // half, mine_ref[k % half], other_ref[k % half]) * scale
        a_ref[p, row:row + 128, column:column + 128] = block + damp if p in diagonal and row == column else block

    def column_step(j, _):
        p = j * n - (j * (j - 1)) // 2
        d = a_ref.at[p]
        d21 = d[128:256, 0:128]
        i11 = inverse_128(d[0:128, 0:128])
        x = dot(d21, i11, NN)
        i22 = inverse_128(d[128:256, 128:256] - dot(x, d21, NT))
        u = dot(i22, x, NN)
        d_ref[j, 0:128, 0:128] = i11 + dot(x, u, TN)
        d_ref[j, 128:256, 0:128] = -u
        d_ref[j, 0:128, 128:256] = -u.T
        d_ref[j, 128:256, 128:256] = i22

        def row_step(i, _):
            panel = dot(a_ref[p + i - j], d_ref[j], NN)
            l_ref[p + i - j] = panel

            def block_step(c, _):
                q = c * n - (c * (c - 1)) // 2 + i - c
                a_ref[q] = a_ref[q] - dot(panel, a_ref[p + c - j], NT)
                return 0

            lax.fori_loop(j + 1, i + 1, block_step, 0)
            return 0

        lax.fori_loop(j + 1, n, row_step, 0)
        return 0

    lax.fori_loop(0, n, column_step, 0)


def factor(core, mine, other, n, scale):
    blocks = n * (n + 1) // 2
    whole = pl.BlockSpec(memory_space=pltpu.VMEM)
    return pl.pallas_call(
        functools.partial(factor_kernel, n, scale),
        out_shape=(
            jax.ShapeDtypeStruct((blocks, 256, 256), jnp.float32),
            jax.ShapeDtypeStruct((n, 256, 256), jnp.float32),
        ),
        in_specs=[pl.BlockSpec(memory_space=pltpu.SMEM), whole, whole],
        out_specs=(whole,) * 2,
        scratch_shapes=[pltpu.VMEM((blocks, 256, 256), jnp.float32)],
        compiler_params=pltpu.CompilerParams(vmem_limit_bytes=20 * MIB),
        cost_estimate=cost(32 * (256 * n) ** 3, 6 * MIB),
    )(core, mine, other)


def solve_kernel(n, scale, t_ref, l_ref, d_ref, wh_ref, wl_ref):
    place = lambda i, j: j * n - j * (j - 1) // 2 + (i - j)
    at = lambda j: slice(256 * j, 256 * j + 256)
    ys = []
    for j in range(n):
        acc = t_ref[:, at(j)]
        for i in range(j):
            acc = acc - dot3(ys[i], split(l_ref[place(j, i)]), NT)
        ys.append(split(acc))
    ws = [None] * n
    for j in reversed(range(n)):
        acc = dot3(ys[j], split(d_ref[j]), NN)
        for i in range(j + 1, n):
            acc = acc - dot3(ws[i], split(l_ref[place(i, j)]), NN)
        ws[j] = split(acc)
        wh_ref[:, at(j)] = ws[j][0] * jnp.bfloat16(scale)
        wl_ref[:, at(j)] = ws[j][1] * jnp.bfloat16(scale)


def solve(t, l, d, n):
    m, features = t.shape
    whole = pl.BlockSpec(memory_space=pltpu.VMEM)
    return pl.pallas_call(
        functools.partial(solve_kernel, n, features ** -0.5),
        out_shape=(jax.ShapeDtypeStruct((m, features), jnp.bfloat16),) * 2,
        in_specs=[whole] * 3,
        out_specs=(whole,) * 2,
        compiler_params=pltpu.CompilerParams(vmem_limit_bytes=36 * MIB),
        cost_estimate=cost(6 * m * features * features, 12 * MIB),
    )(t, l, d)


def score_kernel(pick_ref, wh_ref, wl_ref, v_ref, out_ref):
    step = pl.program_id(0)
    leads, groups = v_ref.shape[:2]
    rows = []
    for s in range(2 * leads):
        pick = pick_ref[step * 2 * leads + s]
        live = (pick >= 0).astype(jnp.float32)
        for y in range(groups):
            rows.append(v_ref[s % leads, y, jnp.maximum(pick, 0)] * live)
    v = split(jnp.concatenate(rows, axis=0))
    out_ref[...] = dot3((wh_ref[...], wl_ref[...]), v, NT)


def score(pick, wh, wl, v, leads):
    m, features = wh.shape
    total, groups, both, part, _ = v.shape
    width = 2 * leads * groups * part
    whole = pl.BlockSpec(memory_space=pltpu.VMEM)
    return pl.pallas_call(
        score_kernel,
        grid=(total // leads,),
        out_shape=jax.ShapeDtypeStruct((m, total * 2 * groups * part), jnp.float32),
        in_specs=[
            pl.BlockSpec(memory_space=pltpu.SMEM),
            whole, whole,
            pl.BlockSpec((leads, groups, both, part, features), lambda i: (i, 0, 0, 0, 0)),
        ],
        out_specs=pl.BlockSpec((m, width), lambda i: (0, i)),
        compiler_params=pltpu.CompilerParams(vmem_limit_bytes=44 * MIB),
        cost_estimate=cost(12 * m * total * groups * part * features, 20 * MIB),
    )(pick, wh, wl, v)


def swap(v):
    return lax.ppermute(v, "core", [(0, 1), (1, 0)])


def ring(v, axis, k):
    size = lax.axis_size(axis)
    return lax.ppermute(v, axis, [(i, (i + k) % size) for i in range(size)])


def scatter(v, axis):
    size, me = lax.axis_size(axis), lax.axis_index(axis)
    part = lambda k: lax.dynamic_index_in_dim(v, lax.rem(me + k, size), 0, keepdims=False)
    total = part(0)
    for k in range(1, size):
        total = total + ring(part(k), axis, k)
    return total


def gather(v, axis):
    size, me = lax.axis_size(axis), lax.axis_index(axis)
    came = [ring(v, axis, k) for k in range(1, size)]
    out = lax.dynamic_update_index_in_dim(jnp.zeros((size,) + v.shape, v.dtype), v, me, 0)
    for k in range(1, size):
        out = lax.dynamic_update_index_in_dim(out, came[k - 1], lax.rem(me + size - k, size), 0)
    return out


def sum_all(mine, other, beside):
    shape = mine.shape
    ny, nx, nz = lax.axis_size("y"), lax.axis_size("x"), lax.axis_size(Z)
    v = (mine + swap(other)).reshape(ny, nx, -1, 128)
    v, beside = lax.optimization_barrier((scatter(v, "y"), beside))
    v = scatter(v, "x")
    hop = 1
    while hop < nz:
        v = v + lax.ppermute(v, Z, [(i, i ^ hop) for i in range(nz)])
        hop *= 2
    return gather(gather(v, "x"), "y").reshape(shape), beside


def local(train_grads, val_grads, wanted, owner):
    m, features = train_grads.shape
    n = features // 256
    dp = Z + ("x", "core")
    slabs, group = lax.axis_size(dp), lax.axis_size("y")
    plane = slabs // lax.axis_size(Z)
    blocks, part, _ = val_grads.shape

    near = lax.ppermute(val_grads, "z_low", [(0, 1), (1, 0)])
    held = jnp.concatenate([val_grads, near])

    positions = jnp.arange(slabs, dtype=jnp.int32)
    holder = jnp.sum(jnp.where(owner == lax.axis_index(dp), positions, 0))
    request = lax.dynamic_index_in_dim(wanted, holder, 0, keepdims=False)
    apart = ((positions // plane) & 1) ^ lax.axis_index("z_low")
    pick = jnp.where(request >= 0, apart * blocks + request - positions * blocks, -1)

    core = lax.axis_index("core").reshape(1)
    mine, other = gram(core, train_grads, n)
    mine, other, held = lax.optimization_barrier((mine, other, held))
    val_all = lax.all_gather(held, ("z_high", "x", "core", "y"), tiled=False)
    val_all = val_all.reshape(slabs // 2, group, 2 * blocks, part, features)
    mine, pick = sum_all(mine, other, pick)
    l, d = factor(core, mine, swap(mine), n, 1.0 / (m * slabs * group))
    wh, wl = solve(train_grads, l, d, n)
    return score(pick, wh, wl, val_all, plane)


def solution(mesh):
    axes = Z + ("x", "core", "y")
    fine = Mesh(mesh.devices.reshape(4, 2, 4, 2, 4), axes)
    in_specs = (P(axes, None), P(Z + ("x", "core"), "y", None), P(), P())
    return jax.shard_map(local, mesh=fine, in_specs=in_specs, out_specs=P(axes, None), check_vma=False)
```

```python
import functools
import jax
import jax.numpy as jnp
from jax import lax
from jax.experimental import pallas as pl
from jax.experimental.pallas import tpu as pltpu
from jax.sharding import Mesh, PartitionSpec as P

HIGHEST = lax.Precision.HIGHEST
damping = 0.1
NN = ((1,), (0,))
NT = ((1,), (1,))
TN = ((0,), (0,))
MIB = 1024 * 1024
Z = ("z_high", "z_low")


def cost(flops, size):
    return pl.CostEstimate(flops=flops, bytes_accessed=size, transcendentals=0)


def dot(a, b, dims):
    return lax.dot_general(a, b, (dims, ((), ())), precision=HIGHEST, preferred_element_type=jnp.float32)


def split(x):
    high = x.astype(jnp.bfloat16)
    return high, (x - high.astype(jnp.float32)).astype(jnp.bfloat16)


def dot3(a, b, dims):
    d = lambda u, v: lax.dot_general(u, v, (dims, ((), ())), preferred_element_type=jnp.float32)
    return d(a[0], b[1]) + d(a[1], b[0]) + d(a[0], b[0])


def thirds(x):
    high = x.astype(jnp.bfloat16).astype(jnp.float32)
    rest = x - high
    middle = rest.astype(jnp.bfloat16).astype(jnp.float32)
    return high, middle, rest - middle


def inverse_128(matrix):
    width = 2
    pivots = 8 * width
    rows = [matrix[8 * r:8 * r + 8, :] for r in range(16)]
    lane = lax.broadcasted_iota(jnp.int32, (8, 128), 1)
    sub = lax.broadcasted_iota(jnp.int32, (8, 128), 0)
    spread = lambda x, l: jnp.broadcast_to(x[:, l:l + 1], (8, 128))
    row_of = lambda v, i: jnp.broadcast_to(v[i // 8][i % 8:i % 8 + 1, :], (8, 128))
    stack = lambda v: jnp.concatenate(v, axis=0)
    for lo in range(0, 128, pivots):
        first_row = lo // 8
        in_block = (lane >= lo) & (lane < lo + pivots)
        held = rows[first_row:first_row + width]
        cols = [[spread(h, lo + i) for h in held] for i in range(pivots)]
        z = [jnp.where(in_block, (lane - lo == sub + 8 * t).astype(jnp.float32), held[t]) for t in range(width)]
        for i in range(0, pivots, 2):
            one, two = cols[i], cols[i + 1]
            a, b, c = row_of(one, i), row_of(two, i), row_of(two, i + 1)
            r = pl.reciprocal(a * c - b * b)
            at = i // 8
            at_i, at_j = sub == i % 8, sub == i % 8 + 1
            both = at_i | at_j
            m0, m1 = list(one), list(two)
            m0[at] = jnp.where(at_i, -1.0, jnp.where(at_j, 0.0, one[at]))
            m1[at] = jnp.where(at_j, -1.0, jnp.where(at_i, 0.0, two[at]))
            e0 = [x * c - y * b for x, y in zip(m0, m1)]
            e1 = [y * a - x * b for x, y in zip(m0, m1)]

            def step(v):
                ri, rj = row_of(v, i) * r, row_of(v, i + 1) * r
                kept = [jnp.where(both, 0.0, v[t]) if t == at else v[t] for t in range(width)]
                return [kept[t] - (e0[t] * ri + e1[t] * rj) for t in range(width)]

            z = step(z)
            for j in range(i + 2, pivots):
                cols[j] = step(cols[j])
        z = [jnp.where(in_block, -v, v) for v in z]
        z_rows = [row_of(z, i) for i in range(pivots)]
        order = [(first_row + width + r) % 16 for r in range(16 - width)]
        for r in order[:width]:
            terms = [spread(rows[r], lo + i) * z_rows[i] for i in range(pivots)]
            while len(terms) > 1:
                terms = [terms[2 * t] + terms[2 * t + 1] for t in range(len(terms) // 2)]
            rows[r] = jnp.where(in_block, 0.0, rows[r]) - terms[0]
        h, m, l = thirds(stack(held))
        zh, zm, zl = thirds(stack(z))
        left = stack([h, h, m, m, h, l]).astype(jnp.bfloat16)
        right = stack([zh, zm, zh, zm, zl, zh]).astype(jnp.bfloat16)
        change = lax.dot_general(left, right, (TN, ((), ())), preferred_element_type=jnp.float32)
        for r in order[width:]:
            rows[r] = jnp.where(in_block, 0.0, rows[r]) - change[8 * r:8 * r + 8]
        rows[first_row:first_row + width] = z
    return -stack(rows)


def small_blocks(n):
    out, place = [], 0
    for j in range(n):
        for i in range(j, n):
            out += [(place, 0, 0), (place, 128, 0)] + ([(place, 0, 128)] if i > j else []) + [(place, 128, 128)]
            place += 1
    return out


def gram_kernel(n, core_ref, t_ref, mine_ref, other_ref, th_ref, tl_ref, halves_ref):
    core = core_ref[0]
    for j in range(n):
        at = slice(256 * j, 256 * j + 256)
        high, low = split(t_ref[:, at])
        th_ref[at, :] = high.T
        tl_ref[at, :] = low.T
    list_of = small_blocks(n)
    half = len(list_of) // 2
    place = 0
    for j in range(n):
        right = split(t_ref[:, 256 * j:256 * j + 256])
        for i in range(j, n):
            of = slice(256 * i, 256 * i + 256)
            block = dot3((th_ref[of, :], tl_ref[of, :]), right, NN)
            for k, (p, row, column) in enumerate(list_of):
                if p == place:
                    halves_ref[core ^ (k // half), k % half] = block[row:row + 128, column:column + 128]
            place += 1
    mine_ref[...] = halves_ref[0]
    other_ref[...] = halves_ref[1]


def gram(core, t, n):
    m, features = t.shape
    half = len(small_blocks(n)) // 2
    whole = pl.BlockSpec(memory_space=pltpu.VMEM)
    return pl.pallas_call(
        functools.partial(gram_kernel, n),
        out_shape=(jax.ShapeDtypeStruct((half, 128, 128), jnp.float32),) * 2,
        in_specs=[pl.BlockSpec(memory_space=pltpu.SMEM), whole],
        out_specs=(whole,) * 2,
        scratch_shapes=[pltpu.VMEM((features, m), jnp.bfloat16)] * 2 + [pltpu.VMEM((2, half, 128, 128), jnp.float32)],
        compiler_params=pltpu.CompilerParams(vmem_limit_bytes=28 * MIB),
        cost_estimate=cost(6 * m * features * features, 7 * MIB),
    )(core, t)


def factor_kernel(n, scale, core_ref, mine_ref, other_ref, l_ref, d_ref, a_ref):
    core = core_ref[0]
    list_of = small_blocks(n)
    half = len(list_of) // 2
    eye = lax.broadcasted_iota(jnp.int32, (128, 128), 0) == lax.broadcasted_iota(jnp.int32, (128, 128), 1)
    damp = damping * eye.astype(jnp.float32)
    diagonal = [j * n - j * (j - 1) // 2 for j in range(n)]
    for k, (p, row, column) in enumerate(list_of):
        block = jnp.where(core == k // half, mine_ref[k % half], other_ref[k % half]) * scale
        a_ref[p, row:row + 128, column:column + 128] = block + damp if p in diagonal and row == column else block

    def column_step(j, _):
        p = j * n - (j * (j - 1)) // 2
        d = a_ref.at[p]
        d21 = d[128:256, 0:128]
        i11 = inverse_128(d[0:128, 0:128])
        x = dot(d21, i11, NN)
        i22 = inverse_128(d[128:256, 128:256] - dot(x, d21, NT))
        u = dot(i22, x, NN)
        d_ref[j, 0:128, 0:128] = i11 + dot(x, u, TN)
        d_ref[j, 128:256, 0:128] = -u
        d_ref[j, 0:128, 128:256] = -u.T
        d_ref[j, 128:256, 128:256] = i22

        def row_step(i, _):
            panel = dot(a_ref[p + i - j], d_ref[j], NN)
            l_ref[p + i - j] = panel

            def block_step(c, _):
                q = c * n - (c * (c - 1)) // 2 + i - c
                a_ref[q] = a_ref[q] - dot(panel, a_ref[p + c - j], NT)
                return 0

            lax.fori_loop(j + 1, i + 1, block_step, 0)
            return 0

        lax.fori_loop(j + 1, n, row_step, 0)
        return 0

    lax.fori_loop(0, n, column_step, 0)


def factor(core, mine, other, n, scale):
    blocks = n * (n + 1) // 2
    whole = pl.BlockSpec(memory_space=pltpu.VMEM)
    return pl.pallas_call(
        functools.partial(factor_kernel, n, scale),
        out_shape=(
            jax.ShapeDtypeStruct((blocks, 256, 256), jnp.float32),
            jax.ShapeDtypeStruct((n, 256, 256), jnp.float32),
        ),
        in_specs=[pl.BlockSpec(memory_space=pltpu.SMEM), whole, whole],
        out_specs=(whole,) * 2,
        scratch_shapes=[pltpu.VMEM((blocks, 256, 256), jnp.float32)],
        compiler_params=pltpu.CompilerParams(vmem_limit_bytes=20 * MIB),
        cost_estimate=cost(32 * (256 * n) ** 3, 6 * MIB),
    )(core, mine, other)


def solve_kernel(n, scale, t_ref, l_ref, d_ref, wh_ref, wl_ref):
    place = lambda i, j: j * n - j * (j - 1) // 2 + (i - j)
    at = lambda j: slice(256 * j, 256 * j + 256)
    ys = []
    for j in range(n):
        acc = t_ref[:, at(j)]
        for i in range(j):
            acc = acc - dot3(ys[i], split(l_ref[place(j, i)]), NT)
        ys.append(split(acc))
    ws = [None] * n
    for j in reversed(range(n)):
        acc = dot3(ys[j], split(d_ref[j]), NN)
        for i in range(j + 1, n):
            acc = acc - dot3(ws[i], split(l_ref[place(i, j)]), NN)
        ws[j] = split(acc)
        wh_ref[:, at(j)] = ws[j][0] * jnp.bfloat16(scale)
        wl_ref[:, at(j)] = ws[j][1] * jnp.bfloat16(scale)


def solve(t, l, d, n):
    m, features = t.shape
    whole = pl.BlockSpec(memory_space=pltpu.VMEM)
    return pl.pallas_call(
        functools.partial(solve_kernel, n, features ** -0.5),
        out_shape=(jax.ShapeDtypeStruct((m, features), jnp.bfloat16),) * 2,
        in_specs=[whole] * 3,
        out_specs=(whole,) * 2,
        compiler_params=pltpu.CompilerParams(vmem_limit_bytes=36 * MIB),
        cost_estimate=cost(6 * m * features * features, 12 * MIB),
    )(t, l, d)


def score_kernel(pick_ref, wh_ref, wl_ref, v_ref, out_ref):
    step = pl.program_id(0)
    leads, groups = v_ref.shape[:2]
    rows = []
    for s in range(2 * leads):
        pick = pick_ref[step * 2 * leads + s]
        live = (pick >= 0).astype(jnp.float32)
        for y in range(groups):
            rows.append(v_ref[s % leads, y, jnp.maximum(pick, 0)] * live)
    v = split(jnp.concatenate(rows, axis=0))
    out_ref[...] = dot3((wh_ref[...], wl_ref[...]), v, NT)


def score(pick, wh, wl, v, leads):
    m, features = wh.shape
    total, groups, both, part, _ = v.shape
    width = 2 * leads * groups * part
    whole = pl.BlockSpec(memory_space=pltpu.VMEM)
    return pl.pallas_call(
        score_kernel,
        grid=(total // leads,),
        out_shape=jax.ShapeDtypeStruct((m, total * 2 * groups * part), jnp.float32),
        in_specs=[
            pl.BlockSpec(memory_space=pltpu.SMEM),
            whole, whole,
            pl.BlockSpec((leads, groups, both, part, features), lambda i: (i, 0, 0, 0, 0)),
        ],
        out_specs=pl.BlockSpec((m, width), lambda i: (0, i)),
        compiler_params=pltpu.CompilerParams(vmem_limit_bytes=36 * MIB),
        cost_estimate=cost(12 * m * total * groups * part * features, 20 * MIB),
    )(pick, wh, wl, v)


def swap(v):
    return lax.ppermute(v, "core", [(0, 1), (1, 0)])


def ring(v, axis, k):
    size = lax.axis_size(axis)
    return lax.ppermute(v, axis, [(i, (i + k) % size) for i in range(size)])


def scatter(v, axis):
    size, me = lax.axis_size(axis), lax.axis_index(axis)
    part = lambda k: lax.dynamic_index_in_dim(v, lax.rem(me + k, size), 0, keepdims=False)
    total = part(0)
    for k in range(1, size):
        total = total + ring(part(k), axis, k)
    return total


def gather(v, axis):
    size, me = lax.axis_size(axis), lax.axis_index(axis)
    came = [ring(v, axis, k) for k in range(1, size)]
    out = lax.dynamic_update_index_in_dim(jnp.zeros((size,) + v.shape, v.dtype), v, me, 0)
    for k in range(1, size):
        out = lax.dynamic_update_index_in_dim(out, came[k - 1], lax.rem(me + size - k, size), 0)
    return out


def sum_all(mine, other, beside):
    shape = mine.shape
    ny, nx, nz = lax.axis_size("y"), lax.axis_size("x"), lax.axis_size(Z)
    v = (mine + swap(other)).reshape(ny, nx, -1, 128)
    v, beside = lax.optimization_barrier((scatter(v, "y"), beside))
    v = scatter(v, "x")
    across = lambda hop: lax.ppermute(v, Z, [(i, i ^ hop) for i in range(nz)])
    v = (v + across(nz // 2)) + (across(2) + across(nz - 2)) if nz == 8 else lax.psum(v, "z_high")
    v = v + across(1)
    return gather(gather(v, "x"), "y").reshape(shape), beside


def local(train_grads, val_grads, wanted, owner):
    m, features = train_grads.shape
    n = features // 256
    dp = Z + ("x", "core")
    slabs, group = lax.axis_size(dp), lax.axis_size("y")
    plane = slabs // lax.axis_size(Z)
    blocks, part, _ = val_grads.shape

    near = lax.ppermute(val_grads, "z_low", [(0, 1), (1, 0)])
    held = jnp.concatenate([val_grads, near])

    positions = jnp.arange(slabs, dtype=jnp.int32)
    holder = jnp.sum(jnp.where(owner == lax.axis_index(dp), positions, 0))
    request = lax.dynamic_index_in_dim(wanted, holder, 0, keepdims=False)
    apart = ((positions // plane) & 1) ^ lax.axis_index("z_low")
    pick = jnp.where(request >= 0, apart * blocks + request - positions * blocks, -1)

    core = lax.axis_index("core").reshape(1)
    held, core = lax.optimization_barrier((held, core))
    mine, other = gram(core, train_grads, n)
    val_all = lax.all_gather(held, ("z_high", "x", "core", "y"), tiled=False)
    val_all = val_all.reshape(slabs // 2, group, 2 * blocks, part, features)
    mine, pick = sum_all(mine, other, pick)
    l, d = factor(core, mine, swap(mine), n, 1.0 / (m * slabs * group))
    wh, wl = solve(train_grads, l, d, n)
    return score(pick, wh, wl, val_all, plane)


def solution(mesh):
    axes = Z + ("x", "core", "y")
    fine = Mesh(mesh.devices.reshape(4, 2, 4, 2, 4), axes)
    in_specs = (P(axes, None), P(Z + ("x", "core"), "y", None), P(), P())
    return jax.shard_map(local, mesh=fine, in_specs=in_specs, out_specs=P(axes, None), check_vma=False)
```

```python
import functools
import jax
import jax.numpy as jnp
from jax import lax
from jax.experimental import pallas as pl
from jax.experimental.pallas import tpu as pltpu
from jax.sharding import Mesh, PartitionSpec as P

HIGHEST = lax.Precision.HIGHEST
damping = 0.1
NN = ((1,), (0,))
NT = ((1,), (1,))
TN = ((0,), (0,))
MIB = 1024 * 1024
Z = ("z_high", "z_low")


def cost(flops, size):
    return pl.CostEstimate(flops=flops, bytes_accessed=size, transcendentals=0)


def dot(a, b, dims):
    return lax.dot_general(a, b, (dims, ((), ())), precision=HIGHEST, preferred_element_type=jnp.float32)


def split(x):
    high = x.astype(jnp.bfloat16)
    return high, (x - high.astype(jnp.float32)).astype(jnp.bfloat16)


def dot3(a, b, dims):
    d = lambda u, v: lax.dot_general(u, v, (dims, ((), ())), preferred_element_type=jnp.float32)
    return d(a[0], b[1]) + d(a[1], b[0]) + d(a[0], b[0])


def thirds(x):
    high = x.astype(jnp.bfloat16).astype(jnp.float32)
    rest = x - high
    middle = rest.astype(jnp.bfloat16).astype(jnp.float32)
    return high, middle, rest - middle


def inverse_128(matrix):
    width = 2
    pivots = 8 * width
    rows = [matrix[8 * r:8 * r + 8, :] for r in range(16)]
    lane = lax.broadcasted_iota(jnp.int32, (8, 128), 1)
    sub = lax.broadcasted_iota(jnp.int32, (8, 128), 0)
    spread = lambda x, l: jnp.broadcast_to(x[:, l:l + 1], (8, 128))
    row_of = lambda v, i: jnp.broadcast_to(v[i // 8][i % 8:i % 8 + 1, :], (8, 128))
    stack = lambda v: jnp.concatenate(v, axis=0)
    for lo in range(0, 128, pivots):
        first_row = lo // 8
        in_block = (lane >= lo) & (lane < lo + pivots)
        held = rows[first_row:first_row + width]
        cols = [[spread(h, lo + i) for h in held] for i in range(pivots)]
        z = [jnp.where(in_block, (lane - lo == sub + 8 * t).astype(jnp.float32), held[t]) for t in range(width)]
        for i in range(0, pivots, 2):
            one, two = cols[i], cols[i + 1]
            a, b, c = row_of(one, i), row_of(two, i), row_of(two, i + 1)
            r = pl.reciprocal(a * c - b * b)
            at = i // 8
            at_i, at_j = sub == i % 8, sub == i % 8 + 1
            both = at_i | at_j
            m0, m1 = list(one), list(two)
            m0[at] = jnp.where(at_i, -1.0, jnp.where(at_j, 0.0, one[at]))
            m1[at] = jnp.where(at_j, -1.0, jnp.where(at_i, 0.0, two[at]))
            e0 = [x * c - y * b for x, y in zip(m0, m1)]
            e1 = [y * a - x * b for x, y in zip(m0, m1)]

            def step(v):
                ri, rj = row_of(v, i) * r, row_of(v, i + 1) * r
                kept = [jnp.where(both, 0.0, v[t]) if t == at else v[t] for t in range(width)]
                return [kept[t] - (e0[t] * ri + e1[t] * rj) for t in range(width)]

            z = step(z)
            for j in range(i + 2, pivots):
                cols[j] = step(cols[j])
        z = [jnp.where(in_block, -v, v) for v in z]
        z_rows = [row_of(z, i) for i in range(pivots)]
        order = [(first_row + width + r) % 16 for r in range(16 - width)]
        for r in order[:width]:
            terms = [spread(rows[r], lo + i) * z_rows[i] for i in range(pivots)]
            while len(terms) > 1:
                terms = [terms[2 * t] + terms[2 * t + 1] for t in range(len(terms) // 2)]
            rows[r] = jnp.where(in_block, 0.0, rows[r]) - terms[0]
        h, m, l = thirds(stack(held))
        zh, zm, zl = thirds(stack(z))
        left = stack([h, h, m, m, h, l]).astype(jnp.bfloat16)
        right = stack([zh, zm, zh, zm, zl, zh]).astype(jnp.bfloat16)
        change = lax.dot_general(left, right, (TN, ((), ())), preferred_element_type=jnp.float32)
        for r in order[width:]:
            rows[r] = jnp.where(in_block, 0.0, rows[r]) - change[8 * r:8 * r + 8]
        rows[first_row:first_row + width] = z
    return -stack(rows)


def small_blocks(n):
    out, place = [], 0
    for j in range(n):
        for i in range(j, n):
            out += [(place, 0, 0), (place, 128, 0)] + ([(place, 0, 128)] if i > j else []) + [(place, 128, 128)]
            place += 1
    return out


def gram_kernel(n, core_ref, t_ref, mine_ref, other_ref, th_ref, tl_ref, halves_ref):
    core = core_ref[0]
    for j in range(n):
        at = slice(256 * j, 256 * j + 256)
        high, low = split(t_ref[:, at])
        th_ref[at, :] = high.T
        tl_ref[at, :] = low.T
    list_of = small_blocks(n)
    half = len(list_of) // 2
    place = 0
    for j in range(n):
        right = split(t_ref[:, 256 * j:256 * j + 256])
        for i in range(j, n):
            of = slice(256 * i, 256 * i + 256)
            block = dot3((th_ref[of, :], tl_ref[of, :]), right, NN)
            for k, (p, row, column) in enumerate(list_of):
                if p == place:
                    halves_ref[core ^ (k // half), k % half] = block[row:row + 128, column:column + 128]
            place += 1
    mine_ref[...] = halves_ref[0]
    other_ref[...] = halves_ref[1]


def gram(core, t, n):
    m, features = t.shape
    half = len(small_blocks(n)) // 2
    whole = pl.BlockSpec(memory_space=pltpu.VMEM)
    return pl.pallas_call(
        functools.partial(gram_kernel, n),
        out_shape=(jax.ShapeDtypeStruct((half, 128, 128), jnp.float32),) * 2,
        in_specs=[pl.BlockSpec(memory_space=pltpu.SMEM), whole],
        out_specs=(whole,) * 2,
        scratch_shapes=[pltpu.VMEM((features, m), jnp.bfloat16)] * 2 + [pltpu.VMEM((2, half, 128, 128), jnp.float32)],
        compiler_params=pltpu.CompilerParams(vmem_limit_bytes=28 * MIB),
        cost_estimate=cost(6 * m * features * features, 7 * MIB),
    )(core, t)


def factor_kernel(n, scale, core_ref, mine_ref, other_ref, l_ref, d_ref, a_ref):
    core = core_ref[0]
    list_of = small_blocks(n)
    half = len(list_of) // 2
    eye = lax.broadcasted_iota(jnp.int32, (128, 128), 0) == lax.broadcasted_iota(jnp.int32, (128, 128), 1)
    damp = damping * eye.astype(jnp.float32)
    diagonal = [j * n - j * (j - 1) // 2 for j in range(n)]
    for k, (p, row, column) in enumerate(list_of):
        block = jnp.where(core == k // half, mine_ref[k % half], other_ref[k % half]) * scale
        a_ref[p, row:row + 128, column:column + 128] = block + damp if p in diagonal and row == column else block

    def column_step(j, _):
        p = j * n - (j * (j - 1)) // 2
        d = a_ref.at[p]
        d21 = d[128:256, 0:128]
        i11 = inverse_128(d[0:128, 0:128])
        x = dot(d21, i11, NN)
        i22 = inverse_128(d[128:256, 128:256] - dot(x, d21, NT))
        u = dot(i22, x, NN)
        d_ref[j, 0:128, 0:128] = i11 + dot(x, u, TN)
        d_ref[j, 128:256, 0:128] = -u
        d_ref[j, 0:128, 128:256] = -u.T
        d_ref[j, 128:256, 128:256] = i22

        def row_step(i, _):
            panel = dot(a_ref[p + i - j], d_ref[j], NN)
            l_ref[p + i - j] = panel

            def block_step(c, _):
                q = c * n - (c * (c - 1)) // 2 + i - c
                a_ref[q] = a_ref[q] - dot(panel, a_ref[p + c - j], NT)
                return 0

            lax.fori_loop(j + 1, i + 1, block_step, 0)
            return 0

        lax.fori_loop(j + 1, n, row_step, 0)
        return 0

    lax.fori_loop(0, n, column_step, 0)


def factor(core, mine, other, n, scale):
    blocks = n * (n + 1) // 2
    whole = pl.BlockSpec(memory_space=pltpu.VMEM)
    return pl.pallas_call(
        functools.partial(factor_kernel, n, scale),
        out_shape=(
            jax.ShapeDtypeStruct((blocks, 256, 256), jnp.float32),
            jax.ShapeDtypeStruct((n, 256, 256), jnp.float32),
        ),
        in_specs=[pl.BlockSpec(memory_space=pltpu.SMEM), whole, whole],
        out_specs=(whole,) * 2,
        scratch_shapes=[pltpu.VMEM((blocks, 256, 256), jnp.float32)],
        compiler_params=pltpu.CompilerParams(vmem_limit_bytes=20 * MIB),
        cost_estimate=cost(32 * (256 * n) ** 3, 6 * MIB),
    )(core, mine, other)


def solve_kernel(n, scale, t_ref, l_ref, d_ref, w_ref):
    place = lambda i, j: j * n - j * (j - 1) // 2 + (i - j)
    at = lambda j: slice(256 * j, 256 * j + 256)
    ys = []
    for j in range(n):
        acc = t_ref[:, at(j)]
        for i in range(j):
            acc = acc - dot3(ys[i], split(l_ref[place(j, i)]), NT)
        ys.append(split(acc))
    ws = [None] * n
    for j in reversed(range(n)):
        acc = dot3(ys[j], split(d_ref[j]), NN)
        for i in range(j + 1, n):
            acc = acc - dot3(ws[i], split(l_ref[place(i, j)]), NN)
        ws[j] = split(acc)
        w_ref[:, at(j)] = ws[j][0] * jnp.bfloat16(scale)
        w_ref[:, at(n + j)] = ws[j][1] * jnp.bfloat16(scale)


def solve(t, l, d, n):
    m, features = t.shape
    whole = pl.BlockSpec(memory_space=pltpu.VMEM)
    return pl.pallas_call(
        functools.partial(solve_kernel, n, features ** -0.5),
        out_shape=jax.ShapeDtypeStruct((m, 2 * features), jnp.bfloat16),
        in_specs=[whole] * 3,
        out_specs=whole,
        compiler_params=pltpu.CompilerParams(vmem_limit_bytes=36 * MIB),
        cost_estimate=cost(6 * m * features * features, 12 * MIB),
    )(t, l, d)


def score_kernel(pick_ref, w_ref, v_ref, out_ref):
    step = pl.program_id(0)
    leads, groups = v_ref.shape[:2]
    rows = []
    for s in range(2 * leads):
        pick = pick_ref[step * 2 * leads + s]
        live = (pick >= 0).astype(jnp.float32)
        for y in range(groups):
            rows.append(v_ref[s % leads, y, jnp.maximum(pick, 0)] * live)
    v = split(jnp.concatenate(rows, axis=0))
    features = v_ref.shape[-1]
    out_ref[...] = dot3((w_ref[:, :features], w_ref[:, features:]), v, NT)


def score(pick, w, v, leads):
    m, features = w.shape[0], v.shape[-1]
    total, groups, both, part, _ = v.shape
    width = 2 * leads * groups * part
    whole = pl.BlockSpec(memory_space=pltpu.VMEM)
    return pl.pallas_call(
        score_kernel,
        grid=(total // leads,),
        out_shape=jax.ShapeDtypeStruct((m, total * 2 * groups * part), jnp.float32),
        in_specs=[
            pl.BlockSpec(memory_space=pltpu.SMEM),
            whole,
            pl.BlockSpec((leads, groups, both, part, features), lambda i: (i, 0, 0, 0, 0)),
        ],
        out_specs=pl.BlockSpec((m, width), lambda i: (0, i)),
        compiler_params=pltpu.CompilerParams(vmem_limit_bytes=36 * MIB),
        cost_estimate=cost(12 * m * total * groups * part * features, 20 * MIB),
    )(pick, w, v)


def swap(v):
    return lax.ppermute(v, "core", [(0, 1), (1, 0)])


def ring(v, axis, k):
    size = lax.axis_size(axis)
    return lax.ppermute(v, axis, [(i, (i + k) % size) for i in range(size)])


def scatter(v, axis):
    size, me = lax.axis_size(axis), lax.axis_index(axis)
    part = lambda k: lax.dynamic_index_in_dim(v, lax.rem(me + k, size), 0, keepdims=False)
    total = part(0)
    for k in range(1, size):
        total = total + ring(part(k), axis, k)
    return total


def gather(v, axis):
    size, me = lax.axis_size(axis), lax.axis_index(axis)
    came = [ring(v, axis, k) for k in range(1, size)]
    out = lax.dynamic_update_index_in_dim(jnp.zeros((size,) + v.shape, v.dtype), v, me, 0)
    for k in range(1, size):
        out = lax.dynamic_update_index_in_dim(out, came[k - 1], lax.rem(me + size - k, size), 0)
    return out


def sum_all(mine, other, beside):
    shape = mine.shape
    ny, nx, nz = lax.axis_size("y"), lax.axis_size("x"), lax.axis_size(Z)
    v = (mine + swap(other)).reshape(ny, nx, -1, 128)
    v, beside = lax.optimization_barrier((scatter(v, "y"), beside))
    v = scatter(v, "x")
    hop = nz // 2
    while hop:
        v = v + lax.ppermute(v, Z, [(i, i ^ hop) for i in range(nz)])
        hop //= 2
    return gather(gather(v, "x"), "y").reshape(shape), beside


def local(train_grads, val_grads, wanted, owner):
    m, features = train_grads.shape
    n = features // 256
    dp = Z + ("x", "core")
    slabs, group = lax.axis_size(dp), lax.axis_size("y")
    plane = slabs // lax.axis_size(Z)
    blocks, part, _ = val_grads.shape

    near = lax.ppermute(val_grads, "z_low", [(0, 1), (1, 0)])
    held = jnp.concatenate([val_grads, near])

    positions = jnp.arange(slabs, dtype=jnp.int32)
    holder = jnp.sum(jnp.where(owner == lax.axis_index(dp), positions, 0))
    request = lax.dynamic_index_in_dim(wanted, holder, 0, keepdims=False)
    apart = ((positions // plane) & 1) ^ lax.axis_index("z_low")
    pick = jnp.where(request >= 0, apart * blocks + request - positions * blocks, -1)

    core = lax.axis_index("core").reshape(1)
    mine, other = gram(core, train_grads, n)
    mine, other, held = lax.optimization_barrier((mine, other, held))
    val_all = lax.all_gather(held, ("z_high", "x", "core", "y"), tiled=False)
    val_all = val_all.reshape(slabs // 2, group, 2 * blocks, part, features)
    mine, pick = sum_all(mine, other, pick)
    l, d = factor(core, mine, swap(mine), n, 1.0 / (m * slabs * group))
    return score(pick, solve(train_grads, l, d, n), val_all, plane)


def solution(mesh):
    axes = Z + ("x", "core", "y")
    fine = Mesh(mesh.devices.reshape(4, 2, 4, 2, 4), axes)
    in_specs = (P(axes, None), P(Z + ("x", "core"), "y", None), P(), P())
    return jax.shard_map(local, mesh=fine, in_specs=in_specs, out_specs=P(axes, None), check_vma=False)
```

```python
import functools
import jax
import jax.numpy as jnp
from jax import lax
from jax.experimental import pallas as pl
from jax.experimental.pallas import tpu as pltpu
from jax.sharding import Mesh, PartitionSpec as P

HIGHEST = lax.Precision.HIGHEST
damping = 0.1
NN = ((1,), (0,))
NT = ((1,), (1,))
TN = ((0,), (0,))
MIB = 1024 * 1024
Z = ("z_high", "z_low")


def cost(flops, size):
    return pl.CostEstimate(flops=flops, bytes_accessed=size, transcendentals=0)


def dot(a, b, dims):
    return lax.dot_general(a, b, (dims, ((), ())), precision=HIGHEST, preferred_element_type=jnp.float32)


def split(x):
    high = x.astype(jnp.bfloat16)
    return high, (x - high.astype(jnp.float32)).astype(jnp.bfloat16)


def dot3(a, b, dims):
    d = lambda u, v: lax.dot_general(u, v, (dims, ((), ())), preferred_element_type=jnp.float32)
    return d(a[0], b[1]) + d(a[1], b[0]) + d(a[0], b[0])


def thirds(x):
    high = x.astype(jnp.bfloat16).astype(jnp.float32)
    rest = x - high
    middle = rest.astype(jnp.bfloat16).astype(jnp.float32)
    return high, middle, rest - middle


def inverse_128(matrix):
    width = 2
    pivots = 8 * width
    rows = [matrix[8 * r:8 * r + 8, :] for r in range(16)]
    lane = lax.broadcasted_iota(jnp.int32, (8, 128), 1)
    sub = lax.broadcasted_iota(jnp.int32, (8, 128), 0)
    spread = lambda x, l: jnp.broadcast_to(x[:, l:l + 1], (8, 128))
    row_of = lambda v, i: jnp.broadcast_to(v[i // 8][i % 8:i % 8 + 1, :], (8, 128))
    stack = lambda v: jnp.concatenate(v, axis=0)
    for lo in range(0, 128, pivots):
        first_row = lo // 8
        in_block = (lane >= lo) & (lane < lo + pivots)
        held = rows[first_row:first_row + width]
        cols = [[spread(h, lo + i) for h in held] for i in range(pivots)]
        z = [jnp.where(in_block, (lane - lo == sub + 8 * t).astype(jnp.float32), held[t]) for t in range(width)]
        for i in range(0, pivots, 2):
            one, two = cols[i], cols[i + 1]
            a, b, c = row_of(one, i), row_of(two, i), row_of(two, i + 1)
            r = pl.reciprocal(a * c - b * b)
            at = i // 8
            at_i, at_j = sub == i % 8, sub == i % 8 + 1
            both = at_i | at_j
            m0, m1 = list(one), list(two)
            m0[at] = jnp.where(at_i, -1.0, jnp.where(at_j, 0.0, one[at]))
            m1[at] = jnp.where(at_j, -1.0, jnp.where(at_i, 0.0, two[at]))
            e0 = [x * c - y * b for x, y in zip(m0, m1)]
            e1 = [y * a - x * b for x, y in zip(m0, m1)]

            def step(v):
                ri, rj = row_of(v, i) * r, row_of(v, i + 1) * r
                kept = [jnp.where(both, 0.0, v[t]) if t == at else v[t] for t in range(width)]
                return [kept[t] - (e0[t] * ri + e1[t] * rj) for t in range(width)]

            z = step(z)
            for j in range(i + 2, pivots):
                cols[j] = step(cols[j])
        z = [jnp.where(in_block, -v, v) for v in z]
        z_rows = [row_of(z, i) for i in range(pivots)]
        order = [(first_row + width + r) % 16 for r in range(16 - width)]
        for r in order[:width]:
            terms = [spread(rows[r], lo + i) * z_rows[i] for i in range(pivots)]
            while len(terms) > 1:
                terms = [terms[2 * t] + terms[2 * t + 1] for t in range(len(terms) // 2)]
            rows[r] = jnp.where(in_block, 0.0, rows[r]) - terms[0]
        h, m, l = thirds(stack(held))
        zh, zm, zl = thirds(stack(z))
        left = stack([h, h, m, m, h, l]).astype(jnp.bfloat16)
        right = stack([zh, zm, zh, zm, zl, zh]).astype(jnp.bfloat16)
        change = lax.dot_general(left, right, (TN, ((), ())), preferred_element_type=jnp.float32)
        for r in order[width:]:
            rows[r] = jnp.where(in_block, 0.0, rows[r]) - change[8 * r:8 * r + 8]
        rows[first_row:first_row + width] = z
    return -stack(rows)


def small_blocks(n):
    out, place = [], 0
    for j in range(n):
        for i in range(j, n):
            out += [(place, 0, 0), (place, 128, 0)] + ([(place, 0, 128)] if i > j else []) + [(place, 128, 128)]
            place += 1
    return out


def gram_kernel(n, core_ref, t_ref, mine_ref, other_ref, th_ref, tl_ref, halves_ref):
    core = core_ref[0]
    for j in range(n):
        at = slice(256 * j, 256 * j + 256)
        high, low = split(t_ref[:, at])
        th_ref[at, :] = high.T
        tl_ref[at, :] = low.T
    list_of = small_blocks(n)
    half = len(list_of) // 2
    place = 0
    for j in range(n):
        right = split(t_ref[:, 256 * j:256 * j + 256])
        for i in range(j, n):
            of = slice(256 * i, 256 * i + 256)
            block = dot3((th_ref[of, :], tl_ref[of, :]), right, NN)
            for k, (p, row, column) in enumerate(list_of):
                if p == place:
                    halves_ref[core ^ (k // half), k % half] = block[row:row + 128, column:column + 128]
            place += 1
    mine_ref[...] = halves_ref[0]
    other_ref[...] = halves_ref[1]


def gram(core, t, n):
    m, features = t.shape
    half = len(small_blocks(n)) // 2
    whole = pl.BlockSpec(memory_space=pltpu.VMEM)
    return pl.pallas_call(
        functools.partial(gram_kernel, n),
        out_shape=(jax.ShapeDtypeStruct((half, 128, 128), jnp.float32),) * 2,
        in_specs=[pl.BlockSpec(memory_space=pltpu.SMEM), whole],
        out_specs=(whole,) * 2,
        scratch_shapes=[pltpu.VMEM((features, m), jnp.bfloat16)] * 2 + [pltpu.VMEM((2, half, 128, 128), jnp.float32)],
        compiler_params=pltpu.CompilerParams(vmem_limit_bytes=28 * MIB),
        cost_estimate=cost(6 * m * features * features, 7 * MIB),
    )(core, t)


def factor_kernel(n, scale, core_ref, mine_ref, other_ref, l_ref, d_ref, a_ref):
    core = core_ref[0]
    list_of = small_blocks(n)
    half = len(list_of) // 2
    eye = lax.broadcasted_iota(jnp.int32, (128, 128), 0) == lax.broadcasted_iota(jnp.int32, (128, 128), 1)
    damp = damping * eye.astype(jnp.float32)
    diagonal = [j * n - j * (j - 1) // 2 for j in range(n)]
    for k, (p, row, column) in enumerate(list_of):
        block = jnp.where(core == k // half, mine_ref[k % half], other_ref[k % half]) * scale
        a_ref[p, row:row + 128, column:column + 128] = block + damp if p in diagonal and row == column else block

    def column_step(j, _):
        p = j * n - (j * (j - 1)) // 2
        d = a_ref.at[p]
        d21 = d[128:256, 0:128]
        i11 = inverse_128(d[0:128, 0:128])
        x = dot(d21, i11, NN)
        i22 = inverse_128(d[128:256, 128:256] - dot(x, d21, NT))
        u = dot(i22, x, NN)
        d_ref[j, 0:128, 0:128] = i11 + dot(x, u, TN)
        d_ref[j, 128:256, 0:128] = -u
        d_ref[j, 0:128, 128:256] = -u.T
        d_ref[j, 128:256, 128:256] = i22

        def row_step(i, _):
            panel = dot(a_ref[p + i - j], d_ref[j], NN)
            l_ref[p + i - j] = panel

            def block_step(c, _):
                q = c * n - (c * (c - 1)) // 2 + i - c
                a_ref[q] = a_ref[q] - dot(panel, a_ref[p + c - j], NT)
                return 0

            lax.fori_loop(j + 1, i + 1, block_step, 0)
            return 0

        lax.fori_loop(j + 1, n, row_step, 0)
        return 0

    lax.fori_loop(0, n, column_step, 0)


def factor(core, mine, other, n, scale):
    blocks = n * (n + 1) // 2
    whole = pl.BlockSpec(memory_space=pltpu.VMEM)
    return pl.pallas_call(
        functools.partial(factor_kernel, n, scale),
        out_shape=(
            jax.ShapeDtypeStruct((blocks, 256, 256), jnp.float32),
            jax.ShapeDtypeStruct((n, 256, 256), jnp.float32),
        ),
        in_specs=[pl.BlockSpec(memory_space=pltpu.SMEM), whole, whole],
        out_specs=(whole,) * 2,
        scratch_shapes=[pltpu.VMEM((blocks, 256, 256), jnp.float32)],
        compiler_params=pltpu.CompilerParams(vmem_limit_bytes=20 * MIB),
        cost_estimate=cost(32 * (256 * n) ** 3, 6 * MIB),
    )(core, mine, other)


def solve_kernel(n, scale, t_ref, l_ref, d_ref, wh_ref, wl_ref):
    place = lambda i, j: j * n - j * (j - 1) // 2 + (i - j)
    at = lambda j: slice(256 * j, 256 * j + 256)
    ys = []
    for j in range(n):
        acc = t_ref[:, at(j)]
        for i in range(j):
            acc = acc - dot3(ys[i], split(l_ref[place(j, i)]), NT)
        ys.append(split(acc))
    ws = [None] * n
    for j in reversed(range(n)):
        acc = dot3(ys[j], split(d_ref[j]), NN)
        for i in range(j + 1, n):
            acc = acc - dot3(ws[i], split(l_ref[place(i, j)]), NN)
        ws[j] = split(acc)
        wh_ref[:, at(j)] = ws[j][0] * jnp.bfloat16(scale)
        wl_ref[:, at(j)] = ws[j][1] * jnp.bfloat16(scale)


def solve(t, l, d, n):
    m, features = t.shape
    whole = pl.BlockSpec(memory_space=pltpu.VMEM)
    return pl.pallas_call(
        functools.partial(solve_kernel, n, features ** -0.5),
        out_shape=(jax.ShapeDtypeStruct((m, features), jnp.bfloat16),) * 2,
        in_specs=[whole] * 3,
        out_specs=(whole,) * 2,
        compiler_params=pltpu.CompilerParams(vmem_limit_bytes=36 * MIB),
        cost_estimate=cost(6 * m * features * features, 12 * MIB),
    )(t, l, d)


def score_kernel(pick_ref, wh_ref, wl_ref, v_ref, out_ref):
    step = pl.program_id(0)
    leads, groups = v_ref.shape[:2]
    rows = []
    for s in range(2 * leads):
        pick = pick_ref[step * 2 * leads + s]
        live = (pick >= 0).astype(jnp.float32)
        for y in range(groups):
            rows.append(v_ref[s % leads, y, jnp.maximum(pick, 0)] * live)
    v = split(jnp.concatenate(rows, axis=0))
    out_ref[...] = dot3((wh_ref[...], wl_ref[...]), v, NT)


def score(pick, wh, wl, v, leads):
    m, features = wh.shape
    total, groups, both, part, _ = v.shape
    width = 2 * leads * groups * part
    whole = pl.BlockSpec(memory_space=pltpu.VMEM)
    return pl.pallas_call(
        score_kernel,
        grid=(total // leads,),
        out_shape=jax.ShapeDtypeStruct((m, total * 2 * groups * part), jnp.float32),
        in_specs=[
            pl.BlockSpec(memory_space=pltpu.SMEM),
            whole, whole,
            pl.BlockSpec((leads, groups, both, part, features), lambda i: (i, 0, 0, 0, 0)),
        ],
        out_specs=pl.BlockSpec((m, width), lambda i: (0, i)),
        compiler_params=pltpu.CompilerParams(vmem_limit_bytes=44 * MIB),
        cost_estimate=cost(12 * m * total * groups * part * features, 20 * MIB),
    )(pick, wh, wl, v)


def swap(v):
    return lax.ppermute(v, "core", [(0, 1), (1, 0)])


def ring(v, axis, k):
    size = lax.axis_size(axis)
    return lax.ppermute(v, axis, [(i, (i + k) % size) for i in range(size)])


def scatter(v, axis):
    size, me = lax.axis_size(axis), lax.axis_index(axis)
    part = lambda k: lax.dynamic_index_in_dim(v, lax.rem(me + k, size), 0, keepdims=False)
    total = part(0)
    for k in range(1, size):
        total = total + ring(part(k), axis, k)
    return total


def gather(v, axis):
    size, me = lax.axis_size(axis), lax.axis_index(axis)
    came = [ring(v, axis, k) for k in range(1, size)]
    out = lax.dynamic_update_index_in_dim(jnp.zeros((size,) + v.shape, v.dtype), v, me, 0)
    for k in range(1, size):
        out = lax.dynamic_update_index_in_dim(out, came[k - 1], lax.rem(me + size - k, size), 0)
    return out


def sum_all(mine, other, beside):
    shape = mine.shape
    ny, nx, nz = lax.axis_size("y"), lax.axis_size("x"), lax.axis_size(Z)
    v = (mine + swap(other)).reshape(nx, ny, -1, 128)
    v, beside = lax.optimization_barrier((scatter(v, "x"), beside))
    v = scatter(v, "y")
    hop = 1
    while hop < nz:
        v = v + lax.ppermute(v, Z, [(i, i ^ hop) for i in range(nz)])
        hop *= 2
    return gather(gather(v, "y"), "x").reshape(shape), beside


def local(train_grads, val_grads, wanted, owner):
    m, features = train_grads.shape
    n = features // 256
    dp = Z + ("x", "core")
    slabs, group = lax.axis_size(dp), lax.axis_size("y")
    plane = slabs // lax.axis_size(Z)
    blocks, part, _ = val_grads.shape

    near = lax.ppermute(val_grads, "z_low", [(0, 1), (1, 0)])
    held = jnp.concatenate([val_grads, near])

    positions = jnp.arange(slabs, dtype=jnp.int32)
    holder = jnp.sum(jnp.where(owner == lax.axis_index(dp), positions, 0))
    request = lax.dynamic_index_in_dim(wanted, holder, 0, keepdims=False)
    apart = ((positions // plane) & 1) ^ lax.axis_index("z_low")
    pick = jnp.where(request >= 0, apart * blocks + request - positions * blocks, -1)

    core = lax.axis_index("core").reshape(1)
    mine, other = gram(core, train_grads, n)
    mine, other, held = lax.optimization_barrier((mine, other, held))
    val_all = lax.all_gather(held, ("z_high", "x", "core", "y"), tiled=False)
    val_all = val_all.reshape(slabs // 2, group, 2 * blocks, part, features)
    mine, pick = sum_all(mine, other, pick)
    l, d = factor(core, mine, swap(mine), n, 1.0 / (m * slabs * group))
    wh, wl = solve(train_grads, l, d, n)
    return score(pick, wh, wl, val_all, plane)


def solution(mesh):
    axes = Z + ("x", "core", "y")
    fine = Mesh(mesh.devices.reshape(4, 2, 4, 2, 4), axes)
    in_specs = (P(axes, None), P(Z + ("x", "core"), "y", None), P(), P())
    return jax.shard_map(local, mesh=fine, in_specs=in_specs, out_specs=P(axes, None), check_vma=False)
```
